256 devices in a mesh: rows: 128 (over z, y, x), feat: 2 (over core).
Axes of the slice: x: 4, y: 4, z: 8, core: 2. Of those that a mesh axis runs over, the one named last changes fastest.
Arguments:
- student: bfloat16 [40960, 1024], P('rows', 'feat')
- teacher: bfloat16 [40960, 1536], P('rows', 'feat')
- rounds: int32 [4], replicated, may hold values from 1 to 127
Outputs:
- student_grad: float32 [40960, 1024], P('rows', 'feat')
- loss: float32 [], replicated
The draws below stay inside these ranges and needn't reach their ends.
Inputs may be any that keep to these rules, and one draw needn't show every extreme that they name: Round r pairs block b with block b XOR rounds[r].
All inputs are finite; a program needn't handle non-finite values.
Results may differ from the reference program's by a relative error of at most 0.018.
Values may be sent and summed in bfloat16 or wider, within the bound.
A program may use at most 64 MiB of HBM per device.

```python
import math
import jax
import jax.numpy as jnp
from jax import lax

DS = 1024
DT = 1536
ROW_DEV = 320
ROUNDS = 4
N_ROWS = 128


def class_labels(key):
    count = ROW_DEV * N_ROWS
    return jax.random.randint(jax.random.fold_in(key, 5), (count,), 0, 256)


def scaled_rows(key, labels, width, common_part, class_part, noise_part, top_scale):
    common_key, centre_key, noise_key, scale_key = jax.random.split(key, 4)
    count = ROW_DEV * N_ROWS
    ramp = 1.0 + 2.0 * jnp.arange(count, dtype=jnp.float32)[:, None] / float(count - 1)
    common = jnp.clip(jax.random.normal(common_key, (1, width), jnp.float32), -4.0, 4.0)
    centres = jnp.clip(jax.random.normal(centre_key, (256, width), jnp.float32), -4.0, 4.0)
    noise = jnp.clip(jax.random.normal(noise_key, (count, width), jnp.float32), -6.0, 6.0)
    spread = jnp.exp(jax.random.uniform(scale_key, (count, 1), jnp.float32, 0.0, math.log(top_scale)))
    rows = common_part * common + class_part * centres[labels] + noise_part * noise
    return rows * spread * ramp * 0.5


def draw_student(key, part):
    labels = class_labels(key)
    key = jax.random.fold_in(key, 11)
    rows = scaled_rows(key, labels, DS, 0.5, 0.6, 0.62, 4.0)
    return rows.astype(jnp.bfloat16)


def draw_teacher(key, part):
    labels = class_labels(key)
    key = jax.random.fold_in(key, 23)
    rows = scaled_rows(key, labels, DT, 0.5, 0.6, 0.62, 4.0)
    return rows.astype(jnp.bfloat16)


def plant(entries, rng, smallest, top_value):
    extent = entries.shape
    place = [jax.random.randint(jax.random.fold_in(rng, axis), (), 0, extent[axis]) for axis in range(len(extent))]
    entries = entries.at[tuple(place)].set(smallest)
    longest = extent.index(max(extent))
    place[longest] = (place[longest] + 1) % extent[longest]
    return entries.at[tuple(place)].set(top_value)


def setup_inputs(seed: int = 0) -> dict:
    arg_keys = jax.random.split(jax.random.key(seed), 4)
    return {
        "student": draw_student(jax.random.fold_in(arg_keys[3], 71), 0),
        "teacher": draw_teacher(jax.random.fold_in(arg_keys[3], 71), 0),
        "rounds": plant(jax.random.randint(arg_keys[2], (ROUNDS,), 1, N_ROWS), jax.random.fold_in(arg_keys[2], 1), 1, N_ROWS - 1).astype(jnp.int32),
    }


def block_rows(data, index):
    start = (index * ROW_DEV).astype(jnp.int32)
    return lax.dynamic_slice_in_dim(data, start, ROW_DEV, 0)

def distances(left, right):
    left_sq = lax.optimization_barrier(jnp.sum(left.astype(jnp.float32) ** 2, axis=1))
    right_sq = lax.optimization_barrier(jnp.sum(right.astype(jnp.float32) ** 2, axis=1))
    inner = jnp.dot(left, right.T, preferred_element_type=jnp.float32)
    return jnp.sqrt(left_sq[:, None] + right_sq[None, :] - 2.0 * inner + 1.0)

def partners(block, rounds):
    others = jnp.bitwise_xor(block, rounds).astype(jnp.int32)
    return jnp.concatenate([jnp.reshape(block, (1,)).astype(jnp.int32), others])

def tile_pairs(student, teacher, rounds, block):
    own_s = block_rows(student, block)
    own_t = block_rows(teacher, block)
    result = []
    mates = partners(block, rounds)
    for slot in range(ROUNDS + 1):
        mate_s = block_rows(student, mates[slot])
        mate_t = block_rows(teacher, mates[slot])
        result.append((own_s, mate_s, distances(own_s, mate_s), distances(own_t, mate_t)))
    return result

def reference(student, teacher, rounds):
    pair_count = float(N_ROWS * (ROUNDS + 1) * ROW_DEV * ROW_DEV)
    blocks = jnp.arange(N_ROWS, dtype=jnp.int32)

    def first_pass(block):
        total_s = jnp.zeros((), jnp.float32)
        total_t = jnp.zeros((), jnp.float32)
        for own_s, mate_s, dist_s, dist_t in tile_pairs(student, teacher, rounds, block):
            total_s = total_s + jnp.sum(dist_s)
            total_t = total_t + jnp.sum(dist_t)
        return (total_s, total_t)
    sums_s, sums_t = lax.map(first_pass, blocks)
    mean_s = jnp.sum(sums_s) / pair_count
    mean_t = jnp.sum(sums_t) / pair_count

    def second_pass(block):
        total_h = jnp.zeros((), jnp.float32)
        total_g = jnp.zeros((), jnp.float32)
        for own_s, mate_s, dist_s, dist_t in tile_pairs(student, teacher, rounds, block):
            err = dist_s / mean_s - dist_t / mean_t
            huber = jnp.where(jnp.abs(err) < 1.0, 0.5 * err * err, jnp.abs(err) - 0.5)
            slope = jnp.clip(err, -1.0, 1.0)
            total_h = total_h + jnp.sum(huber)
            total_g = total_g + jnp.sum(slope * dist_s)
        return (total_h, total_g)
    sums_h, sums_g = lax.map(second_pass, blocks)
    loss = jnp.sum(sums_h) / pair_count
    kappa = jnp.sum(sums_g) / (mean_s * pair_count)

    def third_pass(block):
        grad = jnp.zeros((ROW_DEV, DS), jnp.float32)
        for own_s, mate_s, dist_s, dist_t in tile_pairs(student, teacher, rounds, block):
            err = dist_s / mean_s - dist_t / mean_t
            slope = jnp.clip(err, -1.0, 1.0)
            weight = (slope - kappa) / dist_s
            row_total = lax.optimization_barrier(jnp.sum(weight, axis=1))
            pulled = jnp.dot(weight.astype(jnp.bfloat16), mate_s, preferred_element_type=jnp.float32)
            grad = grad + row_total[:, None] * own_s.astype(jnp.float32) - pulled
        return 2.0 * grad
    grads = lax.map(third_pass, blocks)
    return (jnp.reshape(grads, (N_ROWS * ROW_DEV, DS)), loss)
```

```python
import functools
import jax
import jax.numpy as jnp
from jax import lax
from jax.experimental import pallas as pl
from jax.experimental.pallas import tpu as pltpu
from jax.sharding import PartitionSpec as P

MESH = pl.DeviceIdType.MESH
F32 = jnp.float32
BF16 = jnp.bfloat16
NZ = 8
NP = 16
ROWS = 320
HALF = 160
CR = 80
CC = 128
ROUNDS = 4
TILES = ROUNDS + 1
SQ = 512
UQ = 256


def nt_dot(a, b):
    return lax.dot_general(a, b, (((1,), (1,)), ((), ())), preferred_element_type=F32)


def col_norms(m):
    x = m.astype(F32)
    sq = x * x
    hi = sq.astype(BF16)
    lo = (sq - hi.astype(F32)).astype(BF16)
    ones = jnp.ones((8, m.shape[1]), BF16)
    return (nt_dot(ones, hi) + nt_dot(ones, lo))[0:1, :]


def row_norms(m):
    x = m.astype(F32)
    return jnp.sum(x * x, axis=1, keepdims=True)


def wait_bytes(ref, sem):
    pltpu.make_async_copy(ref, ref, sem).wait()


def kernel(pairs, rounds_ref, s_ref, t_ref, grad_ref, loss_ref,
           gs, gt, gu, stage_s, stage_t, stage_u, ms, mt, mu,
           rn_s, rn_t, ds, dt, xs, xt, ys, yt, wb, rsum, pv, pa, pb,
           p1_send, p1_recv, ring_send, ring_recv, p2_send, p2_recv,
           x_send, x_recv, w_send, w_recv, r_send, r_recv, ps_send, ps_recv):
    row = lax.axis_index("rows")
    core = lax.axis_index("feat")
    z = row // NP
    me = row % NP
    other = 1 - core
    holder = (me // 8) == core
    base = z * NP

    def plane(d):
        return {"rows": base + d}

    def line(q):
        return {"rows": (q % NZ) * NP + me, "feat": q // NZ}

    q_me = core * NZ + z
    right = {"rows": ((z + 1) % NZ) * NP + me}
    left = {"rows": ((z + NZ - 1) % NZ) * NP + me}
    mate_core = {"feat": other}

    barrier = pltpu.get_barrier_semaphore()

    def greet(k, carry):
        pl.semaphore_signal(barrier, inc=1, device_id=plane((me + k) % NP), device_id_type=MESH)
        pl.semaphore_signal(barrier, inc=1, device_id=line((q_me + k) % NP), device_id_type=MESH)
        return carry
    lax.fori_loop(1, NP, greet, 0)
    pl.semaphore_wait(barrier, 2 * (NP - 1))

    def rect(ref, i, first=0):
        r0 = pl.multiple_of((i % 4) * CR, 16)
        c0 = pl.multiple_of(first + (i // 4) * CC, CC)
        return ref.at[pl.ds(r0, CR), pl.ds(c0, CC)]

    def scatter(src, g, slot):
        def one(k, carry):
            d = (me + k) % NP
            pltpu.make_async_remote_copy(
                rect(src, d), g.at[z, me], p1_send.at[slot], p1_recv.at[slot],
                device_id=plane(d), device_id_type=MESH).start()
            return carry
        lax.fori_loop(1, NP, one, 0)
        pltpu.make_async_copy(rect(src, me), g.at[z, me], p1_recv.at[slot]).start()

    def scatter_u():
        def one(j, carry):
            d = core * 8 + j

            @pl.when(d != me)
            def _():
                pltpu.make_async_remote_copy(
                    rect(t_ref, j, SQ), gu.at[z, me], p1_send.at[2], p1_recv.at[2],
                    device_id=plane(d), device_id_type=MESH).start()
            return carry
        lax.fori_loop(0, 8, one, 0)

        @pl.when(holder)
        def _():
            pltpu.make_async_copy(rect(t_ref, me % 8, SQ), gu.at[z, me], p1_recv.at[2]).start()

    def ring_pair(g, slot, step):
        br = (z + NZ - step) % NZ
        bl = (z + step) % NZ
        r_ref, l_ref = g.at[br], g.at[bl]
        if step == NZ // 2 - 1:
            r_ref = r_ref.at[pl.ds(0, NP // 2)]
            l_ref = l_ref.at[pl.ds(NP // 2, NP // 2)]
        a = pltpu.make_async_remote_copy(
            r_ref, r_ref, ring_send.at[slot, 0, step], ring_recv.at[slot, 0, step],
            device_id=right, device_id_type=MESH)
        b = pltpu.make_async_remote_copy(
            l_ref, l_ref, ring_send.at[slot, 1, step], ring_recv.at[slot, 1, step],
            device_id=left, device_id_type=MESH)
        return a, b

    def ring_start(g, slot, step):
        if step > 0:
            a, b = ring_pair(g, slot, step - 1)
            a.wait_recv()
            b.wait_recv()
        if step < NZ // 2:
            a, b = ring_pair(g, slot, step)
            a.start()
            b.start()

    def ring_flush(g, slot):
        for step in range(NZ // 2):
            a, b = ring_pair(g, slot, step)
            a.wait_send()
            b.wait_send()

    def deliver(g, stage, mate, slot, r, i):
        mask = rounds_ref[r]
        zz = z ^ (mask // NP)
        low = mask % NP

        def one(d, carry):
            stage[r, d] = g[zz, d ^ low]

            @pl.when(d != me)
            def _():
                pltpu.make_async_remote_copy(
                    stage.at[r, d], rect(mate.at[r], i), p2_send.at[slot, r], p2_recv.at[slot, r],
                    device_id=plane(d), device_id_type=MESH).start()

            @pl.when(d == me)
            def _():
                pltpu.make_async_copy(stage.at[r, d], rect(mate.at[r], i), p2_recv.at[slot, r]).start()
            return carry
        lax.fori_loop(0, NP, one, 0)

    own_rows = pl.ds(pl.multiple_of(core * HALF, 16), HALF)
    far_rows = pl.ds(pl.multiple_of(other * HALF, 16), HALF)

    def cross(x, y, side, k):
        return pltpu.make_async_remote_copy(
            x.at[k], y.at[k], x_send.at[side, k], x_recv.at[side, k],
            device_id=mate_core, device_id_type=MESH)

    def tile_s(k, m):
        cn = col_norms(m)
        xs[k] = rn_s[far_rows, 0:1] + cn - 2.0 * nt_dot(s_ref[far_rows, :], m)
        cross(xs, ys, 0, k).start()
        ds[k] = rn_s[own_rows, 0:1] + cn - 2.0 * nt_dot(s_ref[own_rows, :], m)

    def tile_t(k, m):
        cn = col_norms(m)
        xt[k] = rn_t[far_rows, 0:1] + cn - 2.0 * nt_dot(t_ref[far_rows, 0:SQ], m)
        dt[k] = rn_t[own_rows, 0:1] + cn - 2.0 * nt_dot(t_ref[own_rows, 0:SQ], m)

    def tile_u(k, m):
        cn = col_norms(m)
        xt[k] += cn - 2.0 * nt_dot(t_ref[far_rows, SQ:SQ + UQ], m)
        cross(xt, yt, 1, k).start()
        dt[k] += cn - 2.0 * nt_dot(t_ref[own_rows, SQ:SQ + UQ], m)

    def finish(d, x, y, side):
        def one(k, acc):
            cross(x, y, side, k).wait_recv()
            v = jnp.sqrt(d[k] + y[k] + 1.0)
            d[k] = v
            return acc + jnp.sum(v, axis=0, keepdims=True)
        acc = lax.fori_loop(0, TILES, one, jnp.zeros((1, ROWS), F32))
        return jnp.sum(acc, axis=1, keepdims=True)

    def all_sum(n, a, b):
        first = lax.broadcasted_iota(jnp.int32, (8, 128), 0) == 0
        v = jnp.where(first, a, b)
        pv[n, 0] = v
        pa[n, me] = v

        def send_a(k, carry):
            pltpu.make_async_remote_copy(
                pv.at[n, 0], pa.at[n, me], ps_send.at[n, 0], ps_recv.at[n, 0],
                device_id=plane((me + k) % NP), device_id_type=MESH).start()
            return carry
        lax.fori_loop(1, NP, send_a, 0)
        wait_bytes(pa.at[n, pl.ds(0, NP - 1)], ps_recv.at[n, 0])
        v = jnp.sum(pa[n], axis=0)
        pv[n, 1] = v
        pb[n, q_me] = v

        def send_b(k, carry):
            pltpu.make_async_remote_copy(
                pv.at[n, 1], pb.at[n, q_me], ps_send.at[n, 1], ps_recv.at[n, 1],
                device_id=line((q_me + k) % NP), device_id_type=MESH).start()
            return carry
        lax.fori_loop(1, NP, send_b, 0)
        wait_bytes(pb.at[n, pl.ds(0, NP - 1)], ps_recv.at[n, 1])
        v = jnp.sum(pb[n], axis=0)
        return v[0:1, 0:1], v[1:2, 0:1]

    scatter(s_ref, gs, 0)
    rn_s[...] = jnp.broadcast_to(row_norms(s_ref[...]), (ROWS, 128))
    wait_bytes(gs.at[z], p1_recv.at[0])
    ring_start(gs, 0, 0)
    scatter(t_ref, gt, 1)
    scatter_u()
    rn_t[...] = jnp.broadcast_to(row_norms(t_ref[...]), (ROWS, 128))
    wait_bytes(gt.at[z], p1_recv.at[1])
    ring_start(gt, 1, 0)
    tile_s(0, s_ref[...])
    ring_start(gs, 0, 1)
    tile_t(0, t_ref[:, 0:SQ])
    ring_start(gs, 0, 2)
    tile_u(0, t_ref[:, SQ:SQ + UQ])
    ring_start(gs, 0, 3)

    ring_start(gt, 1, 1)

    @pl.when(holder)
    def _():
        wait_bytes(gu.at[z], p1_recv.at[2])
        ring_start(gu, 2, 0)
    ring_start(gs, 0, 4)
    deliver(gs, stage_s, ms, 0, 0, me)
    deliver(gs, stage_s, ms, 0, 1, me)
    ring_start(gt, 1, 2)
    deliver(gs, stage_s, ms, 0, 2, me)
    deliver(gs, stage_s, ms, 0, 3, me)
    ring_start(gt, 1, 3)

    @pl.when(holder)
    def _():
        ring_start(gu, 2, 1)

    def mate_s(r, carry):
        wait_bytes(ms.at[r], p2_recv.at[0, r])
        tile_s(r + 1, ms[r])
        return carry
    lax.fori_loop(0, 2, mate_s, 0)

    @pl.when(holder)
    def _():
        ring_start(gu, 2, 2)
    ring_start(gt, 1, 4)
    for r in range(ROUNDS):
        deliver(gt, stage_t, mt, 1, r, me)

    @pl.when(holder)
    def _():
        ring_start(gu, 2, 3)
    lax.fori_loop(2, ROUNDS, mate_s, 0)

    @pl.when(holder)
    def _():
        ring_start(gu, 2, 4)
        for r in range(ROUNDS):
            deliver(gu, stage_u, mu, 2, r, me % 8)

    sum_s = finish(ds, xs, ys, 0)

    def mate_t(r, carry):
        wait_bytes(mt.at[r], p2_recv.at[1, r])
        tile_t(r + 1, mt[r])
        return carry
    lax.fori_loop(0, ROUNDS, mate_t, 0)

    def mate_u(r, carry):
        wait_bytes(mu.at[r], p2_recv.at[2, r])
        tile_u(r + 1, mu[r])
        return carry
    lax.fori_loop(0, ROUNDS, mate_u, 0)
    sum_t = finish(dt, xt, yt, 1)

    total_s, total_t = all_sum(0, sum_s, sum_t)
    mean_s = total_s / pairs
    mean_t = total_t / pairs
    inv_s = 1.0 / mean_s
    inv_t = 1.0 / mean_t

    def second(k, carry):
        h, g = carry
        d = ds[k]
        err = d * inv_s - dt[k] * inv_t
        size = jnp.abs(err)
        slope = jnp.clip(err, -1.0, 1.0)
        hub = jnp.where(size < 1.0, 0.5 * err * err, size - 0.5)
        dt[k] = slope
        return (h + jnp.sum(hub, axis=0, keepdims=True),
                g + jnp.sum(slope * d, axis=0, keepdims=True))
    zero = jnp.zeros((1, ROWS), F32)
    acc_h, acc_g = lax.fori_loop(0, TILES, second, (zero, zero))
    total_h, total_g = all_sum(
        1, jnp.sum(acc_h, axis=1, keepdims=True), jnp.sum(acc_g, axis=1, keepdims=True))
    loss_ref[...] = jnp.broadcast_to(total_h / pairs, (8, 128))
    kappa = total_g / (mean_s * pairs)

    def weights_copy(k):
        part = wb.at[k, own_rows]
        return pltpu.make_async_remote_copy(
            part, part, w_send.at[k], w_recv.at[k], device_id=mate_core, device_id_type=MESH)

    def third(k, acc):
        w = (dt[k] - kappa) / ds[k]
        wb[k, own_rows] = w.astype(BF16)
        weights_copy(k).start()
        return acc + jnp.sum(w, axis=1, keepdims=True)
    sums = lax.fori_loop(0, TILES, third, jnp.zeros((HALF, 1), F32))
    rsum[own_rows, :] = jnp.broadcast_to(sums, (HALF, 128))
    sums_copy = pltpu.make_async_remote_copy(
        rsum.at[own_rows], rsum.at[own_rows], r_send, r_recv,
        device_id=mate_core, device_id_type=MESH)
    sums_copy.start()

    weights_copy(0).wait_recv()
    grad_ref[...] = jnp.dot(wb[0], s_ref[...], preferred_element_type=F32)

    def pull(r, carry):
        weights_copy(r + 1).wait_recv()
        grad_ref[...] += jnp.dot(wb[r + 1], ms[r], preferred_element_type=F32)
        return carry
    lax.fori_loop(0, ROUNDS, pull, 0)
    sums_copy.wait_recv()
    grad_ref[...] = 2.0 * (rsum[:, 0:1] * s_ref[...].astype(F32) - grad_ref[...])

    wait_bytes(gs.at[0, pl.ds(0, NP - 1)], p1_send.at[0])
    wait_bytes(gt.at[0, pl.ds(0, NP - 1)], p1_send.at[1])
    ring_flush(gs, 0)
    ring_flush(gt, 1)

    @pl.when(holder)
    def _():
        wait_bytes(gu.at[0, pl.ds(0, 7)], p1_send.at[2])
        ring_flush(gu, 2)
        for r in range(ROUNDS):
            wait_bytes(stage_u.at[r, pl.ds(0, NP - 1)], p2_send.at[2, r])

    @pl.when(jnp.logical_not(holder))
    def _():
        wait_bytes(gu.at[0, pl.ds(0, 8)], p1_send.at[2])
    for r in range(ROUNDS):
        wait_bytes(stage_s.at[r, pl.ds(0, NP - 1)], p2_send.at[0, r])
        wait_bytes(stage_t.at[r, pl.ds(0, NP - 1)], p2_send.at[1, r])
    for k in range(TILES):
        cross(xs, ys, 0, k).wait_send()
        cross(xt, yt, 1, k).wait_send()
        weights_copy(k).wait_send()
    sums_copy.wait_send()
    for n in range(2):
        for half in range(2):
            wait_bytes(pa.at[n, pl.ds(0, NP - 1)], ps_send.at[n, half])


def body(student, teacher, rounds):
    pairs = float(NZ * NP * TILES * ROWS * ROWS)
    vmem = pl.BlockSpec(memory_space=pltpu.VMEM)
    dma = pltpu.SemaphoreType.DMA
    grad, loss = pl.pallas_call(
        functools.partial(kernel, pairs),
        out_shape=(jax.ShapeDtypeStruct((ROWS, SQ), F32), jax.ShapeDtypeStruct((8, 128), F32)),
        in_specs=[pl.BlockSpec(memory_space=pltpu.SMEM), vmem, vmem],
        out_specs=(vmem, vmem),
        scratch_shapes=[
            pltpu.VMEM((NZ, NP, CR, CC), BF16),
            pltpu.VMEM((NZ, NP, CR, CC), BF16),
            pltpu.VMEM((NZ, NP, CR, CC), BF16),
            pltpu.VMEM((ROUNDS, NP, CR, CC), BF16),
            pltpu.VMEM((ROUNDS, NP, CR, CC), BF16),
            pltpu.VMEM((ROUNDS, NP, CR, CC), BF16),
            pltpu.VMEM((ROUNDS, ROWS, SQ), BF16),
            pltpu.VMEM((ROUNDS, ROWS, SQ), BF16),
            pltpu.VMEM((ROUNDS, ROWS, UQ), BF16),
            pltpu.VMEM((ROWS, 128), F32),
            pltpu.VMEM((ROWS, 128), F32),
            pltpu.VMEM((TILES, HALF, ROWS), F32),
            pltpu.VMEM((TILES, HALF, ROWS), F32),
            pltpu.VMEM((TILES, HALF, ROWS), F32),
            pltpu.VMEM((TILES, HALF, ROWS), F32),
            pltpu.VMEM((TILES, HALF, ROWS), F32),
            pltpu.VMEM((TILES, HALF, ROWS), F32),
            pltpu.VMEM((TILES, ROWS, ROWS), BF16),
            pltpu.VMEM((ROWS, 128), F32),
            pltpu.VMEM((2, 2, 8, 128), F32),
            pltpu.VMEM((2, NP, 8, 128), F32),
            pltpu.VMEM((2, NP, 8, 128), F32),
            dma((3,)), dma((3,)),
            dma((3, 2, NZ // 2)), dma((3, 2, NZ // 2)),
            dma((3, ROUNDS)), dma((3, ROUNDS)),
            dma((2, TILES)), dma((2, TILES)),
            dma((TILES,)), dma((TILES,)),
            dma, dma,
            dma((2, 2)), dma((2, 2)),
        ],
        compiler_params=pltpu.CompilerParams(
            collective_id=0, has_side_effects=True, vmem_limit_bytes=56 * 1024 * 1024),
        name="relation",
    )(rounds, student, teacher)
    return grad, loss[0, 0]


def solution(mesh):
    return jax.shard_map(
        body,
        mesh=mesh,
        in_specs=(P("rows", "feat"), P("rows", "feat"), P()),
        out_specs=(P("rows", "feat"), P()),
        check_vma=False,
    )
```

```python
import functools
import jax
import jax.numpy as jnp
from jax import lax
from jax.experimental import pallas as pl
from jax.experimental.pallas import tpu as pltpu
from jax.sharding import PartitionSpec as P

MESH = pl.DeviceIdType.MESH
F32 = jnp.float32
BF16 = jnp.bfloat16
NZ = 8
NP = 16
ROWS = 320
HALF = 160
CR = 80
CC = 128
ROUNDS = 4
TILES = ROUNDS + 1
SQ = 512
UQ = 256
VA = 48
VB = 32
PARTS = 4


def nt_dot(a, b):
    return lax.dot_general(a, b, (((1,), (1,)), ((), ())), preferred_element_type=F32)


def col_norms(m):
    x = m.astype(F32)
    sq = x * x
    hi = sq.astype(BF16)
    lo = (sq - hi.astype(F32)).astype(BF16)
    ones = jnp.ones((8, m.shape[1]), BF16)
    return (nt_dot(ones, hi) + nt_dot(ones, lo))[0:1, :]


def row_norms(m):
    x = m.astype(F32)
    return jnp.sum(x * x, axis=1, keepdims=True)


def wait_bytes(ref, sem):
    pltpu.make_async_copy(ref, ref, sem).wait()


def kernel(pairs, rounds_ref, s_hbm, t_hbm, ga_ref, gb_ref, scal_ref,
           s_ref, t_ref, gs, gu, ga, gb, stage_s, stage_u, stage_a, stage_b, ms, mt, mu,
           rn_s, rn_t, ds, dt, xs, xt, ys, yt, wa, wb, ra, rb, pv, pa, pb,
           in_sem, p1_send, p1_recv, ring_send, ring_recv, p2_send, p2_recv,
           x_send, x_recv, w_send, w_recv, r_send, r_recv, ps_send, ps_recv):
    load_s = pltpu.make_async_copy(s_hbm, s_ref, in_sem.at[0])
    load_t = pltpu.make_async_copy(t_hbm, t_ref, in_sem.at[1])
    load_s.start()
    load_t.start()
    row = lax.axis_index("rows")
    core = lax.axis_index("feat")
    z = row // NP
    me = row % NP
    other = 1 - core
    holder = (me // 8) == core
    base = z * NP

    def plane(d):
        return {"rows": base + d}

    def line(q):
        return {"rows": (q % NZ) * NP + me, "feat": q // NZ}

    q_me = core * NZ + z
    right = {"rows": ((z + 1) % NZ) * NP + me}
    left = {"rows": ((z + NZ - 1) % NZ) * NP + me}
    mate_core = {"feat": other}

    barrier = pltpu.get_barrier_semaphore()

    def greet(k, carry):
        pl.semaphore_signal(barrier, inc=1, device_id=plane((me + k) % NP), device_id_type=MESH)
        pl.semaphore_signal(barrier, inc=1, device_id=line((q_me + k) % NP), device_id_type=MESH)
        return carry
    lax.fori_loop(1, NP, greet, 0)
    load_s.wait()
    rn_s[...] = jnp.broadcast_to(row_norms(s_ref[...]), (ROWS, 128))
    load_t.wait()
    rn_t[...] = jnp.broadcast_to(row_norms(t_ref[...]), (ROWS, 128))
    pl.semaphore_wait(barrier, 2 * (NP - 1))

    S, U, A, B = (0, 0, 0, CR), (1, SQ, 0, CR), (2, 0, 0, VA), (3, 0, VA, VB)

    def rect(ref, i, piece, first=0):
        r0 = pl.multiple_of((i % 4) * CR + piece[2], 16)
        c0 = pl.multiple_of(first + (i // 4) * CC, CC)
        return ref.at[pl.ds(r0, piece[3]), pl.ds(c0, CC)]

    def scatter(src, g, piece):
        slot = piece[0]

        def one(k, carry):
            d = (me + k) % NP
            pltpu.make_async_remote_copy(
                rect(src, d, piece), g.at[z, me], p1_send.at[slot], p1_recv.at[slot],
                device_id=plane(d), device_id_type=MESH).start()
            return carry
        lax.fori_loop(1, NP, one, 0)
        pltpu.make_async_copy(rect(src, me, piece), g.at[z, me], p1_recv.at[slot]).start()

    def scatter_u():
        def one(j, carry):
            d = core * 8 + j

            @pl.when(d != me)
            def _():
                pltpu.make_async_remote_copy(
                    rect(t_ref, j, U, SQ), gu.at[z, me], p1_send.at[1], p1_recv.at[1],
                    device_id=plane(d), device_id_type=MESH).start()
            return carry
        lax.fori_loop(0, 8, one, 0)

        @pl.when(holder)
        def _():
            pltpu.make_async_copy(rect(t_ref, me % 8, U, SQ), gu.at[z, me], p1_recv.at[1]).start()

    def scattered(g, piece):
        wait_bytes(g.at[z], p1_recv.at[piece[0]])

    def ring_copy(g, slot, way, part, step):
        block = (z + NZ - step) % NZ if way == 0 else (z + step) % NZ
        ref = g.at[block, pl.ds(part * (NP // PARTS), NP // PARTS)]
        return pltpu.make_async_remote_copy(
            ref, ref, ring_send.at[slot, way, part, step], ring_recv.at[slot, way, part, step],
            device_id=right if way == 0 else left, device_id_type=MESH)

    def ways(part, step):
        return (0, 1) if step < NZ // 2 - 1 else (part // (PARTS // 2),)

    def ring(g, piece, step, parts=range(PARTS)):
        slot = piece[0]
        for part in parts:
            if step > 0:
                for way in ways(part, step - 1):
                    ring_copy(g, slot, way, part, step - 1).wait_recv()
            if step < NZ // 2:
                for way in ways(part, step):
                    ring_copy(g, slot, way, part, step).start()

    def ring_flush(g, piece):
        for step in range(NZ // 2):
            for part in range(PARTS):
                for way in ways(part, step):
                    ring_copy(g, piece[0], way, part, step).wait_send()

    def ring_u(step):
        @pl.when(holder)
        def _():
            if step == 0:
                scattered(gu, U)
            ring(gu, U, step)

    def deliver(g, stage, mate, piece, r, i):
        slot = piece[0]
        mask = rounds_ref[r]
        zz = z ^ (mask // NP)
        low = mask % NP

        def one(d, carry):
            stage[r, d] = g[zz, d ^ low]

            @pl.when(d != me)
            def _():
                pltpu.make_async_remote_copy(
                    stage.at[r, d], rect(mate.at[r], i, piece), p2_send.at[slot, r], p2_recv.at[slot, r],
                    device_id=plane(d), device_id_type=MESH).start()

            @pl.when(d == me)
            def _():
                pltpu.make_async_copy(stage.at[r, d], rect(mate.at[r], i, piece), p2_recv.at[slot, r]).start()
            return carry
        lax.fori_loop(0, NP, one, 0)

    own_rows = pl.ds(pl.multiple_of(core * HALF, 16), HALF)
    far_rows = pl.ds(pl.multiple_of(other * HALF, 16), HALF)

    def cross(x, y, side, k):
        return pltpu.make_async_remote_copy(
            x.at[k], y.at[k], x_send.at[side, k], x_recv.at[side, k],
            device_id=mate_core, device_id_type=MESH)

    def tile_s(k, m):
        cn = col_norms(m)
        xs[k] = rn_s[far_rows, 0:1] + cn - 2.0 * nt_dot(s_ref[far_rows, :], m)
        cross(xs, ys, 0, k).start()
        ds[k] = rn_s[own_rows, 0:1] + cn - 2.0 * nt_dot(s_ref[own_rows, :], m)

    def tile_u(k, m):
        cn = col_norms(m)
        xt[k] = rn_t[far_rows, 0:1] + cn - 2.0 * nt_dot(t_ref[far_rows, SQ:SQ + UQ], m)
        dt[k] = rn_t[own_rows, 0:1] + cn - 2.0 * nt_dot(t_ref[own_rows, SQ:SQ + UQ], m)

    def tile_t(k, m):
        cn = col_norms(m)
        xt[k] += cn - 2.0 * nt_dot(t_ref[far_rows, 0:SQ], m)
        cross(xt, yt, 1, k).start()
        dt[k] += cn - 2.0 * nt_dot(t_ref[own_rows, 0:SQ], m)

    def finish(d, x, y, side):
        def one(k, acc):
            cross(x, y, side, k).wait_recv()
            v = jnp.sqrt(d[k] + y[k] + 1.0)
            d[k] = v
            return acc + jnp.sum(v, axis=0, keepdims=True)
        acc = lax.fori_loop(0, TILES, one, jnp.zeros((1, ROWS), F32))
        return jnp.sum(acc, axis=1, keepdims=True)

    def sum_first(n, a, b):
        first = lax.broadcasted_iota(jnp.int32, (8, 128), 0) == 0
        v = jnp.where(first, a, b)
        pv[n, 0] = v
        pa[n, me] = v

        def send(k, carry):
            pltpu.make_async_remote_copy(
                pv.at[n, 0], pa.at[n, me], ps_send.at[n, 0], ps_recv.at[n, 0],
                device_id=plane((me + k) % NP), device_id_type=MESH).start()
            return carry
        lax.fori_loop(1, NP, send, 0)

    def sum_second(n):
        wait_bytes(pa.at[n, pl.ds(0, NP - 1)], ps_recv.at[n, 0])
        v = jnp.sum(pa[n], axis=0)
        pv[n, 1] = v
        pb[n, q_me] = v

        def send(k, carry):
            pltpu.make_async_remote_copy(
                pv.at[n, 1], pb.at[n, q_me], ps_send.at[n, 1], ps_recv.at[n, 1],
                device_id=line((q_me + k) % NP), device_id_type=MESH).start()
            return carry
        lax.fori_loop(1, NP, send, 0)

    def sum_result(n):
        wait_bytes(pb.at[n, pl.ds(0, NP - 1)], ps_recv.at[n, 1])
        v = jnp.sum(pb[n], axis=0)
        return v[0:1, 0:1], v[1:2, 0:1]

    def weights_copy(w, side, k):
        part = w.at[k, own_rows]
        return pltpu.make_async_remote_copy(
            part, part, w_send.at[side, k], w_recv.at[side, k],
            device_id=mate_core, device_id_type=MESH)

    def sums_copy(r, side):
        part = r.at[own_rows]
        return pltpu.make_async_remote_copy(
            part, part, r_send.at[side], r_recv.at[side],
            device_id=mate_core, device_id_type=MESH)

    def send_sums(r, side, sums):
        r[own_rows, :] = jnp.broadcast_to(sums, (HALF, 128))
        sums_copy(r, side).start()

    def pull(w, side, r, g_ref):
        weights_copy(w, side, 0).wait_recv()
        sums_copy(r, side).wait_recv()
        g_ref[...] = (r[:, 0:1] * s_ref[...].astype(F32)
                      - jnp.dot(w[0], s_ref[...], preferred_element_type=F32))

        def one(k, carry):
            weights_copy(w, side, k + 1).wait_recv()
            g_ref[...] -= jnp.dot(w[k + 1], ms[k], preferred_element_type=F32)
            return carry
        lax.fori_loop(0, ROUNDS, one, 0)

    def mate_s(r, carry):
        wait_bytes(stage_s.at[r], p2_recv.at[S[0], r])
        tile_s(r + 1, ms[r])
        return carry

    def mate_u(r, carry):
        wait_bytes(mu.at[r], p2_recv.at[U[0], r])
        tile_u(r + 1, mu[r])
        return carry

    def mate_t(r, carry):
        wait_bytes(stage_a.at[r], p2_recv.at[A[0], r])
        wait_bytes(stage_b.at[r], p2_recv.at[B[0], r])
        tile_t(r + 1, mt[r])
        return carry

    def inverse(k, acc):
        v = 1.0 / ds[k]
        xs[k] = v
        wb[k, own_rows] = v.astype(BF16)
        weights_copy(wb, 1, k).start()
        return acc + jnp.sum(v, axis=1, keepdims=True)

    def deliver_u(*turns):
        @pl.when(holder)
        def _():
            for r in turns:
                deliver(gu, stage_u, mu, U, r, me % 8)

    def deliver_s(r):
        deliver(gs, stage_s, ms, S, r, me)

    def deliver_a(r):
        deliver(ga, stage_a, mt, A, r, me)

    def deliver_b(r):
        deliver(gb, stage_b, mt, B, r, me)

    scatter(s_ref, gs, S)
    scattered(gs, S)
    ring(gs, S, 0)
    scatter_u()
    scatter(t_ref, ga, A)
    scatter(t_ref, gb, B)
    tile_s(0, s_ref[...])
    ring(gs, S, 1)
    tile_u(0, t_ref[:, SQ:SQ + UQ])
    tile_t(0, t_ref[:, 0:SQ])
    ring(gs, S, 2)
    ring_u(0)
    ring(gs, S, 3)
    scattered(ga, A)
    ring(ga, A, 0)
    ring_u(1)
    ring(gs, S, 4)
    deliver_s(0)
    ring(ga, A, 1)
    deliver_s(1)
    ring_u(2)
    deliver_s(2)
    ring(ga, A, 2)
    deliver_s(3)
    ring_u(3)
    ring(ga, A, 3)
    scattered(gb, B)
    ring(gb, B, 0)
    ring_u(4)
    deliver_u(0)
    deliver_u(1)
    ring(ga, A, 4)
    deliver_u(2)
    ring(gb, B, 1)
    deliver_u(3)
    deliver_a(0)
    ring(gb, B, 2)
    deliver_a(1)
    deliver_a(2)
    ring(gb, B, 3)
    deliver_a(3)
    lax.fori_loop(0, ROUNDS, mate_s, 0)
    ring(gb, B, 4)
    for r in range(ROUNDS):
        deliver_b(r)
    lax.fori_loop(0, ROUNDS, mate_u, 0)
    sum_s = finish(ds, xs, ys, 0)
    for k in range(TILES):
        cross(xs, ys, 0, k).wait_send()
    send_sums(rb, 1, lax.fori_loop(0, TILES, inverse, jnp.zeros((HALF, 1), F32)))
    pull(wb, 1, rb, gb_ref)
    lax.fori_loop(0, ROUNDS, mate_t, 0)
    sum_t = finish(dt, xt, yt, 1)

    sum_first(0, sum_s, sum_t)
    sum_second(0)
    total_s, total_t = sum_result(0)
    mean_s = total_s / pairs
    inv_s = 1.0 / mean_s
    inv_t = pairs / total_t

    def second(k, carry):
        h, g, acc = carry
        d = ds[k]
        err = d * inv_s - dt[k] * inv_t
        size = jnp.abs(err)
        slope = jnp.clip(err, -1.0, 1.0)
        hub = jnp.where(size < 1.0, 0.5 * err * err, size - 0.5)
        w = slope * xs[k]
        wa[k, own_rows] = w.astype(BF16)
        weights_copy(wa, 0, k).start()
        return (h + jnp.sum(hub, axis=0, keepdims=True),
                g + jnp.sum(slope * d, axis=0, keepdims=True),
                acc + jnp.sum(w, axis=1, keepdims=True))
    zero = jnp.zeros((1, ROWS), F32)
    acc_h, acc_g, sums = lax.fori_loop(0, TILES, second, (zero, zero, jnp.zeros((HALF, 1), F32)))
    sum_first(1, jnp.sum(acc_h, axis=1, keepdims=True), jnp.sum(acc_g, axis=1, keepdims=True))
    send_sums(ra, 0, sums)
    sum_second(1)
    pull(wa, 0, ra, ga_ref)
    total_h, total_g = sum_result(1)
    first = lax.broadcasted_iota(jnp.int32, (8, 128), 0) == 0
    scal_ref[...] = jnp.where(first, total_g / (mean_s * pairs), total_h / pairs)

    for g, piece, stage in ((gs, S, stage_s), (ga, A, stage_a), (gb, B, stage_b)):
        wait_bytes(g.at[0, pl.ds(0, NP - 1)], p1_send.at[piece[0]])
        ring_flush(g, piece)
        for r in range(ROUNDS):
            wait_bytes(stage.at[r, pl.ds(0, NP - 1)], p2_send.at[piece[0], r])

    @pl.when(holder)
    def _():
        wait_bytes(gu.at[0, pl.ds(0, 7)], p1_send.at[U[0]])
        ring_flush(gu, U)
        for r in range(ROUNDS):
            wait_bytes(stage_u.at[r, pl.ds(0, NP - 1)], p2_send.at[U[0], r])

    @pl.when(jnp.logical_not(holder))
    def _():
        wait_bytes(gu.at[0, pl.ds(0, 8)], p1_send.at[U[0]])
    for k in range(TILES):
        cross(xt, yt, 1, k).wait_send()
        weights_copy(wa, 0, k).wait_send()
        weights_copy(wb, 1, k).wait_send()
    sums_copy(ra, 0).wait_send()
    sums_copy(rb, 1).wait_send()
    for n in range(2):
        for half in range(2):
            wait_bytes(pa.at[n, pl.ds(0, NP - 1)], ps_send.at[n, half])


def combine(scal_ref, ga_ref, gb_ref, grad_ref, loss_ref):
    grad_ref[...] = 2.0 * (ga_ref[...] - scal_ref[0, 0] * gb_ref[...])
    loss_ref[0, 0] = scal_ref[1, 0]


def body(student, teacher, rounds):
    pairs = float(NZ * NP * TILES * ROWS * ROWS)
    vmem = pl.BlockSpec(memory_space=pltpu.VMEM)
    smem = pl.BlockSpec(memory_space=pltpu.SMEM)
    hbm = pl.BlockSpec(memory_space=pl.ANY)
    dma = pltpu.SemaphoreType.DMA
    part = jax.ShapeDtypeStruct((ROWS, SQ), F32)
    ga, gb, scal = pl.pallas_call(
        functools.partial(kernel, pairs),
        out_shape=(part, part, jax.ShapeDtypeStruct((8, 128), F32)),
        in_specs=[smem, hbm, hbm],
        out_specs=(vmem, vmem, vmem),
        scratch_shapes=[
            pltpu.VMEM((ROWS, SQ), BF16),
            pltpu.VMEM((ROWS, SQ + UQ), BF16),
            pltpu.VMEM((NZ, NP, CR, CC), BF16),
            pltpu.VMEM((NZ, NP, CR, CC), BF16),
            pltpu.VMEM((NZ, NP, VA, CC), BF16),
            pltpu.VMEM((NZ, NP, VB, CC), BF16),
            pltpu.VMEM((ROUNDS, NP, CR, CC), BF16),
            pltpu.VMEM((ROUNDS, NP, CR, CC), BF16),
            pltpu.VMEM((ROUNDS, NP, VA, CC), BF16),
            pltpu.VMEM((ROUNDS, NP, VB, CC), BF16),
            pltpu.VMEM((ROUNDS, ROWS, SQ), BF16),
            pltpu.VMEM((ROUNDS, ROWS, SQ), BF16),
            pltpu.VMEM((ROUNDS, ROWS, UQ), BF16),
            pltpu.VMEM((ROWS, 128), F32),
            pltpu.VMEM((ROWS, 128), F32),
            pltpu.VMEM((TILES, HALF, ROWS), F32),
            pltpu.VMEM((TILES, HALF, ROWS), F32),
            pltpu.VMEM((TILES, HALF, ROWS), F32),
            pltpu.VMEM((TILES, HALF, ROWS), F32),
            pltpu.VMEM((TILES, HALF, ROWS), F32),
            pltpu.VMEM((TILES, HALF, ROWS), F32),
            pltpu.VMEM((TILES, ROWS, ROWS), BF16),
            pltpu.VMEM((TILES, ROWS, ROWS), BF16),
            pltpu.VMEM((ROWS, 128), F32),
            pltpu.VMEM((ROWS, 128), F32),
            pltpu.VMEM((2, 2, 8, 128), F32),
            pltpu.VMEM((2, NP, 8, 128), F32),
            pltpu.VMEM((2, NP, 8, 128), F32),
            dma((2,)),
            dma((4,)), dma((4,)),
            dma((4, 2, PARTS, NZ // 2)), dma((4, 2, PARTS, NZ // 2)),
            dma((4, ROUNDS)), dma((4, ROUNDS)),
            dma((2, TILES)), dma((2, TILES)),
            dma((2, TILES)), dma((2, TILES)),
            dma((2,)), dma((2,)),
            dma((2, 2)), dma((2, 2)),
        ],
        compiler_params=pltpu.CompilerParams(
            collective_id=0, has_side_effects=True, vmem_limit_bytes=60 * 1024 * 1024),
        name="relation",
    )(rounds, student, teacher)
    grad, loss = pl.pallas_call(
        combine,
        out_shape=(part, jax.ShapeDtypeStruct((1, 1), F32)),
        in_specs=[smem, vmem, vmem],
        out_specs=(vmem, smem),
        name="combine",
    )(scal, ga, gb)
    return grad, loss[0, 0]


def solution(mesh):
    return jax.shard_map(
        body,
        mesh=mesh,
        in_specs=(P("rows", "feat"), P("rows", "feat"), P()),
        out_specs=(P("rows", "feat"), P()),
        check_vma=False,
    )
```

```python
import functools
import jax
import jax.numpy as jnp
from jax import lax
from jax.experimental import pallas as pl
from jax.experimental.pallas import tpu as pltpu
from jax.sharding import PartitionSpec as P

MESH = pl.DeviceIdType.MESH
F32 = jnp.float32
BF16 = jnp.bfloat16
NZ = 8
NP = 16
ROWS = 320
HALF = 160
CR = 80
CC = 128
ROUNDS = 4
TILES = ROUNDS + 1
SQ = 512
UQ = 256
VA = 48
VB = 32
PARTS = 2


def nt_dot(a, b):
    return lax.dot_general(a, b, (((1,), (1,)), ((), ())), preferred_element_type=F32)


def col_norms(m):
    x = m.astype(F32)
    sq = x * x
    hi = sq.astype(BF16)
    lo = (sq - hi.astype(F32)).astype(BF16)
    ones = jnp.ones((8, m.shape[1]), BF16)
    return (nt_dot(ones, hi) + nt_dot(ones, lo))[0:1, :]


def row_norms(m):
    x = m.astype(F32)
    return jnp.sum(x * x, axis=1, keepdims=True)


def wait_bytes(ref, sem):
    pltpu.make_async_copy(ref, ref, sem).wait()


def kernel(pairs, rounds_ref, s_hbm, t_hbm, ga_ref, gb_ref, scal_ref,
           s_ref, t_ref, gs, gr, gu, ga, gb, stage_s, stage_r, stage_u, stage_a, stage_b, ms, mt, mu,
           rn_s, rn_t, ds, dt, xs, xt, ys, yt, wa, wb, ra, rb, pv, pa, pb,
           in_sem, plane_in, p1_send, p1_recv, ring_send, ring_recv, p2_send, p2_recv,
           x_send, x_recv, w_send, w_recv, r_send, r_recv, ps_send, ps_recv):
    load_s = pltpu.make_async_copy(s_hbm, s_ref, in_sem.at[0])
    load_t = pltpu.make_async_copy(t_hbm, t_ref, in_sem.at[1])
    load_s.start()
    load_t.start()
    row = lax.axis_index("rows")
    core = lax.axis_index("feat")
    z = row // NP
    me = row % NP
    other = 1 - core
    holder = (me // 8) == core
    base = z * NP

    def plane(d):
        return {"rows": base + d}

    def line(q):
        return {"rows": (q % NZ) * NP + me, "feat": q // NZ}

    q_me = core * NZ + z
    above = ((z + 1) % NZ) * NP
    below = ((z + NZ - 1) % NZ) * NP
    right = {"rows": above + me}
    left = {"rows": below + me}
    mate_core = {"feat": other}

    barrier = pltpu.get_barrier_semaphore()

    def greet(k, carry):
        pl.semaphore_signal(barrier, inc=1, device_id=plane((me + k) % NP), device_id_type=MESH)
        return carry
    lax.fori_loop(1, NP, greet, 0)
    for peer in (right, left, mate_core):
        pl.semaphore_signal(barrier, inc=1, device_id=peer, device_id_type=MESH)
    load_s.wait()
    rn_s[...] = jnp.broadcast_to(row_norms(s_ref[...]), (ROWS, 128))
    load_t.wait()
    rn_t[...] = jnp.broadcast_to(row_norms(t_ref[...]), (ROWS, 128))
    pl.semaphore_wait(barrier, NP + 2)
    for peer in (right, left):
        pl.semaphore_signal(plane_in, inc=1, device_id=peer, device_id_type=MESH)

    S, R, U, A, B = (0, 0, VA), (1, VA, VB), (2, 0, CR), (3, 0, VA), (4, VA, VB)

    def rect(ref, i, piece, first=0):
        r0 = pl.multiple_of((i % 4) * CR + piece[1], 16)
        c0 = pl.multiple_of(first + (i // 4) * CC, CC)
        return ref.at[pl.ds(r0, piece[2]), pl.ds(c0, CC)]

    def scatter(src, g, piece):
        slot = piece[0]

        def one(k, carry):
            d = (me + k) % NP
            pltpu.make_async_remote_copy(
                rect(src, d, piece), g.at[z, me], p1_send.at[slot], p1_recv.at[slot],
                device_id=plane(d), device_id_type=MESH).start()
            return carry
        lax.fori_loop(1, NP, one, 0)
        pltpu.make_async_copy(rect(src, me, piece), g.at[z, me], p1_recv.at[slot]).start()

    def spread(src, g, piece):
        slot = piece[0]

        def one(k, carry):
            d = (me + k) % NP
            for way, first in ((0, above), (1, below)):
                pltpu.make_async_remote_copy(
                    rect(src, d, piece), g.at[z, me],
                    ring_send.at[slot], ring_recv.at[slot, way, me // (NP // PARTS), 0],
                    device_id={"rows": first + d}, device_id_type=MESH).start()
            return carry
        lax.fori_loop(0, NP, one, 0)

    def scatter_u():
        def one(j, carry):
            d = core * 8 + j

            @pl.when(d != me)
            def _():
                pltpu.make_async_remote_copy(
                    rect(t_ref, j, U, SQ), gu.at[z, me], p1_send.at[U[0]], p1_recv.at[U[0]],
                    device_id=plane(d), device_id_type=MESH).start()
            return carry
        lax.fori_loop(0, 8, one, 0)

        @pl.when(holder)
        def _():
            pltpu.make_async_copy(rect(t_ref, me % 8, U, SQ), gu.at[z, me], p1_recv.at[U[0]]).start()

    def scattered(g, piece):
        wait_bytes(g.at[z], p1_recv.at[piece[0]])

    def ring_copy(g, slot, way, part, step):
        block = (z + NZ - step) % NZ if way == 0 else (z + step) % NZ
        ref = g.at[block, pl.ds(part * (NP // PARTS), NP // PARTS)]
        return pltpu.make_async_remote_copy(
            ref, ref, ring_send.at[slot], ring_recv.at[slot, way, part, step],
            device_id=right if way == 0 else left, device_id_type=MESH)

    def ways(part, step):
        return (0, 1) if step < NZ // 2 - 1 else (part // (PARTS // 2),)

    def ring(g, piece, step, parts=range(PARTS)):
        slot = piece[0]
        for part in parts:
            if step > 0:
                for way in ways(part, step - 1):
                    ring_copy(g, slot, way, part, step - 1).wait_recv()
            if step < NZ // 2:
                for way in ways(part, step):
                    ring_copy(g, slot, way, part, step).start()

    def ring_flush(g, piece):
        wait_bytes(g.at[pl.ds(0, NZ - 1)], ring_send.at[piece[0]])

    def ring_u(step):
        @pl.when(holder)
        def _():
            if step == 0:
                scattered(gu, U)
            ring(gu, U, step)

    def deliver(g, stage, mate, piece, r, i):
        slot = piece[0]
        mask = rounds_ref[r]
        zz = z ^ (mask // NP)
        low = mask % NP

        def one(d, carry):
            stage[r, d] = g[zz, d ^ low]

            @pl.when(d != me)
            def _():
                pltpu.make_async_remote_copy(
                    stage.at[r, d], rect(mate.at[r], i, piece), p2_send.at[slot], p2_recv.at[slot, r],
                    device_id=plane(d), device_id_type=MESH).start()

            @pl.when(d == me)
            def _():
                pltpu.make_async_copy(stage.at[r, d], rect(mate.at[r], i, piece), p2_recv.at[slot, r]).start()
            return carry
        lax.fori_loop(0, NP, one, 0)

    own_rows = pl.ds(pl.multiple_of(core * HALF, 16), HALF)
    far_rows = pl.ds(pl.multiple_of(other * HALF, 16), HALF)

    def cross(x, y, side, k):
        return pltpu.make_async_remote_copy(
            x.at[k], y.at[k], x_send.at[side], x_recv.at[side, k],
            device_id=mate_core, device_id_type=MESH)

    def tile_s(k, m):
        cn = col_norms(m)
        xs[k] = rn_s[far_rows, 0:1] + cn - 2.0 * nt_dot(s_ref[far_rows, :], m)
        cross(xs, ys, 0, k).start()
        ds[k] = rn_s[own_rows, 0:1] + cn - 2.0 * nt_dot(s_ref[own_rows, :], m)

    def tile_u(k, m):
        cn = col_norms(m)
        xt[k] = rn_t[far_rows, 0:1] + cn - 2.0 * nt_dot(t_ref[far_rows, SQ:SQ + UQ], m)
        dt[k] = rn_t[own_rows, 0:1] + cn - 2.0 * nt_dot(t_ref[own_rows, SQ:SQ + UQ], m)

    def tile_t(k, m):
        cn = col_norms(m)
        xt[k] += cn - 2.0 * nt_dot(t_ref[far_rows, 0:SQ], m)
        cross(xt, yt, 1, k).start()
        dt[k] += cn - 2.0 * nt_dot(t_ref[own_rows, 0:SQ], m)

    def finish(d, x, y, side):
        def one(k, acc):
            cross(x, y, side, k).wait_recv()
            v = jnp.sqrt(d[k] + y[k] + 1.0)
            d[k] = v
            return acc + jnp.sum(v, axis=0, keepdims=True)
        acc = lax.fori_loop(0, TILES, one, jnp.zeros((1, ROWS), F32))
        return jnp.sum(acc, axis=1, keepdims=True)

    def sum_first(n, a, b):
        first = lax.broadcasted_iota(jnp.int32, (8, 128), 0) == 0
        v = jnp.where(first, a, b)
        pv[n, 0] = v
        pa[n, me] = v

        def send(k, carry):
            pltpu.make_async_remote_copy(
                pv.at[n, 0], pa.at[n, me], ps_send.at[n, 0], ps_recv.at[n, 0],
                device_id=plane((me + k) % NP), device_id_type=MESH).start()
            return carry
        lax.fori_loop(1, NP, send, 0)

    def sum_second(n):
        wait_bytes(pa.at[n, pl.ds(0, NP - 1)], ps_recv.at[n, 0])
        v = jnp.sum(pa[n], axis=0)
        pv[n, 1] = v
        pb[n, q_me] = v

        def send(k, carry):
            pltpu.make_async_remote_copy(
                pv.at[n, 1], pb.at[n, q_me], ps_send.at[n, 1], ps_recv.at[n, 1],
                device_id=line((q_me + k) % NP), device_id_type=MESH).start()
            return carry
        lax.fori_loop(1, NP, send, 0)

    def sum_result(n):
        wait_bytes(pb.at[n, pl.ds(0, NP - 1)], ps_recv.at[n, 1])
        v = jnp.sum(pb[n], axis=0)
        return v[0:1, 0:1], v[1:2, 0:1]

    def weights_copy(w, side, k):
        part = w.at[k, own_rows]
        return pltpu.make_async_remote_copy(
            part, part, w_send.at[side], w_recv.at[side, k],
            device_id=mate_core, device_id_type=MESH)

    def sums_copy(r, side):
        part = r.at[own_rows]
        return pltpu.make_async_remote_copy(
            part, part, r_send.at[side], r_recv.at[side],
            device_id=mate_core, device_id_type=MESH)

    def send_sums(r, side, sums):
        r[own_rows, :] = jnp.broadcast_to(sums, (HALF, 128))
        sums_copy(r, side).start()

    def pull(w, side, r, g_ref):
        weights_copy(w, side, 0).wait_recv()
        sums_copy(r, side).wait_recv()
        g_ref[...] = (r[:, 0:1] * s_ref[...].astype(F32)
                      - jnp.dot(w[0], s_ref[...], preferred_element_type=F32))

        def one(k, carry):
            weights_copy(w, side, k + 1).wait_recv()
            g_ref[...] -= jnp.dot(w[k + 1], ms[k], preferred_element_type=F32)
            return carry
        lax.fori_loop(0, ROUNDS, one, 0)

    def mate_s(r, carry):
        wait_bytes(stage_s.at[r], p2_recv.at[S[0], r])
        wait_bytes(stage_r.at[r], p2_recv.at[R[0], r])
        tile_s(r + 1, ms[r])
        return carry

    def mate_u(r, carry):
        wait_bytes(mu.at[r], p2_recv.at[U[0], r])
        tile_u(r + 1, mu[r])
        return carry

    def mate_t(r, carry):
        wait_bytes(stage_a.at[r], p2_recv.at[A[0], r])
        wait_bytes(stage_b.at[r], p2_recv.at[B[0], r])
        tile_t(r + 1, mt[r])
        return carry

    def inverse(k, acc):
        v = 1.0 / ds[k]
        xs[k] = v
        wb[k, own_rows] = v.astype(BF16)
        weights_copy(wb, 1, k).start()
        return acc + jnp.sum(v, axis=1, keepdims=True)

    def deliver_u(*turns):
        @pl.when(holder)
        def _():
            for r in turns:
                deliver(gu, stage_u, mu, U, r, me % 8)

    def deliver_s(r):
        deliver(gs, stage_s, ms, S, r, me)

    def deliver_r(r):
        deliver(gr, stage_r, ms, R, r, me)

    def deliver_a(r):
        deliver(ga, stage_a, mt, A, r, me)

    def deliver_b(r):
        deliver(gb, stage_b, mt, B, r, me)

    scatter(s_ref, gs, S)
    scatter(s_ref, gr, R)
    pl.semaphore_wait(plane_in, 2)
    spread(s_ref, gs, S)
    spread(s_ref, gr, R)
    scatter_u()
    scatter(t_ref, ga, A)
    scatter(t_ref, gb, B)
    tile_s(0, s_ref[...])
    tile_u(0, t_ref[:, SQ:SQ + UQ])
    tile_t(0, t_ref[:, 0:SQ])
    ring(gs, S, 1)
    ring(gr, R, 1)
    ring(gs, S, 2)
    ring(gr, R, 2)
    ring(gs, S, 3)
    ring_u(0)
    ring(gs, S, 4)
    scattered(gs, S)
    deliver_s(0)
    deliver_s(1)
    ring(gr, R, 3)
    deliver_s(2)
    ring_u(1)
    deliver_s(3)
    scattered(ga, A)
    ring(ga, A, 0)
    ring(gr, R, 4)
    scattered(gr, R)
    deliver_r(0)
    deliver_r(1)
    ring_u(2)
    deliver_r(2)
    deliver_r(3)
    ring(ga, A, 1)
    ring_u(3)
    ring(ga, A, 2)
    scattered(gb, B)
    ring(gb, B, 0)
    ring_u(4)
    deliver_u(0)
    deliver_u(1)
    ring(ga, A, 3)
    deliver_u(2)
    ring(gb, B, 1)
    deliver_u(3)
    lax.fori_loop(0, ROUNDS, mate_s, 0)
    ring(ga, A, 4)
    deliver_a(0)
    deliver_a(1)
    ring(gb, B, 2)
    deliver_a(2)
    sum_s = finish(ds, xs, ys, 0)
    wait_bytes(xs, x_send.at[0])
    send_sums(rb, 1, lax.fori_loop(0, TILES, inverse, jnp.zeros((HALF, 1), F32)))
    ring(gb, B, 3)
    deliver_a(3)
    lax.fori_loop(0, ROUNDS, mate_u, 0)
    pull(wb, 1, rb, gb_ref)
    ring(gb, B, 4)
    for r in range(ROUNDS):
        deliver_b(r)
    lax.fori_loop(0, ROUNDS, mate_t, 0)
    sum_t = finish(dt, xt, yt, 1)

    sum_first(0, sum_s, sum_t)
    sum_second(0)
    total_s, total_t = sum_result(0)
    mean_s = total_s / pairs
    inv_s = 1.0 / mean_s
    inv_t = pairs / total_t

    def second(k, carry):
        h, g, acc = carry
        d = ds[k]
        err = d * inv_s - dt[k] * inv_t
        size = jnp.abs(err)
        slope = jnp.clip(err, -1.0, 1.0)
        hub = jnp.where(size < 1.0, 0.5 * err * err, size - 0.5)
        w = slope * xs[k]
        wa[k, own_rows] = w.astype(BF16)
        weights_copy(wa, 0, k).start()
        return (h + jnp.sum(hub, axis=0, keepdims=True),
                g + jnp.sum(slope * d, axis=0, keepdims=True),
                acc + jnp.sum(w, axis=1, keepdims=True))
    zero = jnp.zeros((1, ROWS), F32)
    acc_h, acc_g, sums = lax.fori_loop(0, TILES, second, (zero, zero, jnp.zeros((HALF, 1), F32)))
    sum_first(1, jnp.sum(acc_h, axis=1, keepdims=True), jnp.sum(acc_g, axis=1, keepdims=True))
    send_sums(ra, 0, sums)
    sum_second(1)
    pull(wa, 0, ra, ga_ref)
    total_h, total_g = sum_result(1)
    first = lax.broadcasted_iota(jnp.int32, (8, 128), 0) == 0
    scal_ref[...] = jnp.where(first, total_g / (mean_s * pairs), total_h / pairs)

    for g, piece, stage in ((gs, S, stage_s), (gr, R, stage_r), (ga, A, stage_a),
                            (gb, B, stage_b)):
        wait_bytes(g.at[0, pl.ds(0, NP - 1)], p1_send.at[piece[0]])
        ring_flush(g, piece)
        wait_bytes(stage.at[:, pl.ds(0, NP - 1)], p2_send.at[piece[0]])

    @pl.when(holder)
    def _():
        wait_bytes(gu.at[0, pl.ds(0, 7)], p1_send.at[U[0]])
        ring_flush(gu, U)
        wait_bytes(stage_u.at[:, pl.ds(0, NP - 1)], p2_send.at[U[0]])

    @pl.when(jnp.logical_not(holder))
    def _():
        wait_bytes(gu.at[0, pl.ds(0, 8)], p1_send.at[U[0]])
    wait_bytes(xt, x_send.at[1])
    wait_bytes(wa.at[:, own_rows], w_send.at[0])
    wait_bytes(wb.at[:, own_rows], w_send.at[1])
    sums_copy(ra, 0).wait_send()
    sums_copy(rb, 1).wait_send()
    for n in range(2):
        for half in range(2):
            wait_bytes(pa.at[n, pl.ds(0, NP - 1)], ps_send.at[n, half])


def combine(scal_ref, ga_ref, gb_ref, grad_ref, loss_ref):
    grad_ref[...] = 2.0 * (ga_ref[...] - scal_ref[0, 0] * gb_ref[...])
    loss_ref[0, 0] = scal_ref[1, 0]


def body(student, teacher, rounds):
    pairs = float(NZ * NP * TILES * ROWS * ROWS)
    vmem = pl.BlockSpec(memory_space=pltpu.VMEM)
    smem = pl.BlockSpec(memory_space=pltpu.SMEM)
    hbm = pl.BlockSpec(memory_space=pl.ANY)
    dma = pltpu.SemaphoreType.DMA
    part = jax.ShapeDtypeStruct((ROWS, SQ), F32)
    ga, gb, scal = pl.pallas_call(
        functools.partial(kernel, pairs),
        out_shape=(part, part, jax.ShapeDtypeStruct((8, 128), F32)),
        in_specs=[smem, hbm, hbm],
        out_specs=(vmem, vmem, vmem),
        scratch_shapes=[
            pltpu.VMEM((ROWS, SQ), BF16),
            pltpu.VMEM((ROWS, SQ + UQ), BF16),
            pltpu.VMEM((NZ, NP, VA, CC), BF16),
            pltpu.VMEM((NZ, NP, VB, CC), BF16),
            pltpu.VMEM((NZ, NP, CR, CC), BF16),
            pltpu.VMEM((NZ, NP, VA, CC), BF16),
            pltpu.VMEM((NZ, NP, VB, CC), BF16),
            pltpu.VMEM((ROUNDS, NP, VA, CC), BF16),
            pltpu.VMEM((ROUNDS, NP, VB, CC), BF16),
            pltpu.VMEM((ROUNDS, NP, CR, CC), BF16),
            pltpu.VMEM((ROUNDS, NP, VA, CC), BF16),
            pltpu.VMEM((ROUNDS, NP, VB, CC), BF16),
            pltpu.VMEM((ROUNDS, ROWS, SQ), BF16),
            pltpu.VMEM((ROUNDS, ROWS, SQ), BF16),
            pltpu.VMEM((ROUNDS, ROWS, UQ), BF16),
            pltpu.VMEM((ROWS, 128), F32),
            pltpu.VMEM((ROWS, 128), F32),
            pltpu.VMEM((TILES, HALF, ROWS), F32),
            pltpu.VMEM((TILES, HALF, ROWS), F32),
            pltpu.VMEM((TILES, HALF, ROWS), F32),
            pltpu.VMEM((TILES, HALF, ROWS), F32),
            pltpu.VMEM((TILES, HALF, ROWS), F32),
            pltpu.VMEM((TILES, HALF, ROWS), F32),
            pltpu.VMEM((TILES, ROWS, ROWS), BF16),
            pltpu.VMEM((TILES, ROWS, ROWS), BF16),
            pltpu.VMEM((ROWS, 128), F32),
            pltpu.VMEM((ROWS, 128), F32),
            pltpu.VMEM((2, 2, 8, 128), F32),
            pltpu.VMEM((2, NP, 8, 128), F32),
            pltpu.VMEM((2, NP, 8, 128), F32),
            dma((2,)), pltpu.SemaphoreType.REGULAR,
            dma((5,)), dma((5,)),
            dma((5,)), dma((5, 2, PARTS, NZ // 2)),
            dma((5,)), dma((5, ROUNDS)),
            dma((2,)), dma((2, TILES)),
            dma((2,)), dma((2, TILES)),
            dma((2,)), dma((2,)),
            dma((2, 2)), dma((2, 2)),
        ],
        compiler_params=pltpu.CompilerParams(
            collective_id=0, has_side_effects=True, vmem_limit_bytes=60 * 1024 * 1024),
        name="relation",
    )(rounds, student, teacher)
    grad, loss = pl.pallas_call(
        combine,
        out_shape=(part, jax.ShapeDtypeStruct((1, 1), F32)),
        in_specs=[smem, vmem, vmem],
        out_specs=(vmem, smem),
        name="combine",
    )(scal, ga, gb)
    return grad, loss[0, 0]


def solution(mesh):
    return jax.shard_map(
        body,
        mesh=mesh,
        in_specs=(P("rows", "feat"), P("rows", "feat"), P()),
        out_specs=(P("rows", "feat"), P()),
        check_vma=False,
    )
```

```python
import functools
import jax
import jax.numpy as jnp
from jax import lax
from jax.experimental import pallas as pl
from jax.experimental.pallas import tpu as pltpu
from jax.sharding import PartitionSpec as P

MESH = pl.DeviceIdType.MESH
F32 = jnp.float32
BF16 = jnp.bfloat16
NZ = 8
NP = 16
ROWS = 320
HALF = 160
CR = 80
CC = 128
ROUNDS = 4
TILES = ROUNDS + 1
SQ = 512
UQ = 256
VA = 48
VB = 32
PARTS = 2


def nt_dot(a, b):
    return lax.dot_general(a, b, (((1,), (1,)), ((), ())), preferred_element_type=F32)


def col_norms(m):
    x = m.astype(F32)
    sq = x * x
    hi = sq.astype(BF16)
    lo = (sq - hi.astype(F32)).astype(BF16)
    ones = jnp.ones((8, m.shape[1]), BF16)
    return (nt_dot(ones, hi) + nt_dot(ones, lo))[0:1, :]


def row_norms(m):
    x = m.astype(F32)
    return jnp.sum(x * x, axis=1, keepdims=True)


def wait_bytes(ref, sem):
    pltpu.make_async_copy(ref, ref, sem).wait()


def kernel(pairs, rounds_ref, s_hbm, t_hbm, ga_hbm, gb_hbm, scal_ref, ga_ref, gb_ref,
           s_ref, t_ref, gs, gr, gu, ga, gb, stage_s, stage_r, stage_u, stage_a, stage_b, ms, mt, mu,
           rn_s, rn_t, ds, dt, xs, xt, ys, yt, wa, wb, ra, rb, pv, pa, pb,
           in_sem, plane_in, p1_send, p1_recv, ring_send, ring_recv, p2_send, p2_recv,
           x_send, x_recv, w_send, w_recv, r_send, r_recv, ps_send, ps_recv):
    load_s = pltpu.make_async_copy(s_hbm, s_ref, in_sem.at[0])
    load_t = pltpu.make_async_copy(t_hbm, t_ref, in_sem.at[1])
    load_s.start()
    load_t.start()
    row = lax.axis_index("rows")
    core = lax.axis_index("feat")
    z = row // NP
    me = row % NP
    other = 1 - core
    holder = (me // 8) == core
    base = z * NP

    def plane(d):
        return {"rows": base + d}

    def line(q):
        return {"rows": (q % NZ) * NP + me, "feat": q // NZ}

    q_me = core * NZ + z
    above = ((z + 1) % NZ) * NP
    below = ((z + NZ - 1) % NZ) * NP
    right = {"rows": above + me}
    left = {"rows": below + me}
    mate_core = {"feat": other}

    barrier = pltpu.get_barrier_semaphore()

    def greet(k, carry):
        pl.semaphore_signal(barrier, inc=1, device_id=plane((me + k) % NP), device_id_type=MESH)
        return carry
    lax.fori_loop(1, NP, greet, 0)
    for peer in (right, left, mate_core):
        pl.semaphore_signal(barrier, inc=1, device_id=peer, device_id_type=MESH)
    load_s.wait()
    rn_s[...] = jnp.broadcast_to(row_norms(s_ref[...]), (ROWS, 128))
    load_t.wait()
    rn_t[...] = jnp.broadcast_to(row_norms(t_ref[...]), (ROWS, 128))
    pl.semaphore_wait(barrier, NP + 2)
    for peer in (right, left):
        pl.semaphore_signal(plane_in, inc=1, device_id=peer, device_id_type=MESH)

    S, R, U, A, B = (0, 0, VA), (1, VA, VB), (2, 0, CR), (3, 0, VA), (4, VA, VB)

    def rect(ref, i, piece, first=0):
        r0 = pl.multiple_of((i % 4) * CR + piece[1], 16)
        c0 = pl.multiple_of(first + (i // 4) * CC, CC)
        return ref.at[pl.ds(r0, piece[2]), pl.ds(c0, CC)]

    def scatter(src, g, piece):
        slot = piece[0]

        def one(k, carry):
            d = (me + k) % NP
            pltpu.make_async_remote_copy(
                rect(src, d, piece), g.at[z, me], p1_send.at[slot], p1_recv.at[slot],
                device_id=plane(d), device_id_type=MESH).start()
            return carry
        lax.fori_loop(1, NP, one, 0)
        pltpu.make_async_copy(rect(src, me, piece), g.at[z, me], p1_recv.at[slot]).start()

    def spread(src, g, piece):
        slot = piece[0]

        def one(k, carry):
            d = (me + k) % NP
            for way, first in ((0, above), (1, below)):
                pltpu.make_async_remote_copy(
                    rect(src, d, piece), g.at[z, me],
                    ring_send.at[slot], ring_recv.at[slot, way, me // (NP // PARTS), 0],
                    device_id={"rows": first + d}, device_id_type=MESH).start()
            return carry
        lax.fori_loop(0, NP, one, 0)

    def scatter_u():
        def one(j, carry):
            d = core * 8 + j

            @pl.when(d != me)
            def _():
                pltpu.make_async_remote_copy(
                    rect(t_ref, j, U, SQ), gu.at[z, me], p1_send.at[U[0]], p1_recv.at[U[0]],
                    device_id=plane(d), device_id_type=MESH).start()
            return carry
        lax.fori_loop(0, 8, one, 0)

        @pl.when(holder)
        def _():
            pltpu.make_async_copy(rect(t_ref, me % 8, U, SQ), gu.at[z, me], p1_recv.at[U[0]]).start()

    def scattered(g, piece):
        wait_bytes(g.at[z], p1_recv.at[piece[0]])

    def ring_copy(g, slot, way, part, step):
        block = (z + NZ - step) % NZ if way == 0 else (z + step) % NZ
        ref = g.at[block, pl.ds(part * (NP // PARTS), NP // PARTS)]
        return pltpu.make_async_remote_copy(
            ref, ref, ring_send.at[slot], ring_recv.at[slot, way, part, step],
            device_id=right if way == 0 else left, device_id_type=MESH)

    def ways(part, step):
        return (0, 1) if step < NZ // 2 - 1 else (part // (PARTS // 2),)

    def ring(g, piece, step, parts=range(PARTS)):
        slot = piece[0]
        for part in parts:
            if step > 0:
                for way in ways(part, step - 1):
                    ring_copy(g, slot, way, part, step - 1).wait_recv()
            if step < NZ // 2:
                for way in ways(part, step):
                    ring_copy(g, slot, way, part, step).start()

    def ring_flush(g, piece):
        wait_bytes(g.at[pl.ds(0, NZ - 1)], ring_send.at[piece[0]])

    def ring_u(step):
        @pl.when(holder)
        def _():
            if step == 0:
                scattered(gu, U)
            ring(gu, U, step)

    def deliver(g, stage, mate, piece, r, i):
        slot = piece[0]
        mask = rounds_ref[r]
        zz = z ^ (mask // NP)
        low = mask % NP

        def one(d, carry):
            stage[r, d] = g[zz, d ^ low]

            @pl.when(d != me)
            def _():
                pltpu.make_async_remote_copy(
                    stage.at[r, d], rect(mate.at[r], i, piece), p2_send.at[slot], p2_recv.at[slot, r],
                    device_id=plane(d), device_id_type=MESH).start()

            @pl.when(d == me)
            def _():
                pltpu.make_async_copy(stage.at[r, d], rect(mate.at[r], i, piece), p2_recv.at[slot, r]).start()
            return carry
        lax.fori_loop(0, NP, one, 0)

    own_rows = pl.ds(pl.multiple_of(core * HALF, 16), HALF)
    far_rows = pl.ds(pl.multiple_of(other * HALF, 16), HALF)

    def cross(x, y, side, k):
        return pltpu.make_async_remote_copy(
            x.at[k], y.at[k], x_send.at[side], x_recv.at[side, k],
            device_id=mate_core, device_id_type=MESH)

    def tile_s(k, m):
        cn = col_norms(m)
        xs[k] = rn_s[far_rows, 0:1] + cn - 2.0 * nt_dot(s_ref[far_rows, :], m)
        cross(xs, ys, 0, k).start()
        ds[k] = rn_s[own_rows, 0:1] + cn - 2.0 * nt_dot(s_ref[own_rows, :], m)

    def tile_u(k, m):
        cn = col_norms(m)
        xt[k] = rn_t[far_rows, 0:1] + cn - 2.0 * nt_dot(t_ref[far_rows, SQ:SQ + UQ], m)
        dt[k] = rn_t[own_rows, 0:1] + cn - 2.0 * nt_dot(t_ref[own_rows, SQ:SQ + UQ], m)

    def tile_t(k, m):
        cn = col_norms(m)
        xt[k] += cn - 2.0 * nt_dot(t_ref[far_rows, 0:SQ], m)
        cross(xt, yt, 1, k).start()
        dt[k] += cn - 2.0 * nt_dot(t_ref[own_rows, 0:SQ], m)

    def finish(d, x, y, side):
        def one(k, acc):
            cross(x, y, side, k).wait_recv()
            v = jnp.sqrt(d[k] + y[k] + 1.0)
            d[k] = v
            return acc + jnp.sum(v, axis=0, keepdims=True)
        acc = lax.fori_loop(0, TILES, one, jnp.zeros((1, ROWS), F32))
        return jnp.sum(acc, axis=1, keepdims=True)

    def sum_first(n, a, b):
        first = lax.broadcasted_iota(jnp.int32, (1, 128), 1) == 0
        v = jnp.where(first, a, b)
        pv[n, 0] = v
        pa[n, me] = v

        def send(k, carry):
            pltpu.make_async_remote_copy(
                pv.at[n, 0], pa.at[n, me], ps_send.at[n, 0], ps_recv.at[n, 0],
                device_id=plane((me + k) % NP), device_id_type=MESH).start()
            return carry
        lax.fori_loop(1, NP, send, 0)

    def sum_second(n):
        wait_bytes(pa.at[n, pl.ds(0, NP - 1)], ps_recv.at[n, 0])
        v = jnp.sum(pa[n], axis=0)
        pv[n, 1] = v
        pb[n, q_me] = v

        def send(k, carry):
            pltpu.make_async_remote_copy(
                pv.at[n, 1], pb.at[n, q_me], ps_send.at[n, 1], ps_recv.at[n, 1],
                device_id=line((q_me + k) % NP), device_id_type=MESH).start()
            return carry
        lax.fori_loop(1, NP, send, 0)

    def sum_result(n):
        wait_bytes(pb.at[n, pl.ds(0, NP - 1)], ps_recv.at[n, 1])
        v = jnp.sum(pb[n], axis=0)
        return v[:, 0:1], v[:, 1:2]

    def weights_copy(w, side, k):
        part = w.at[k, own_rows]
        return pltpu.make_async_remote_copy(
            part, part, w_send.at[side], w_recv.at[side, k],
            device_id=mate_core, device_id_type=MESH)

    def sums_copy(r, side):
        part = r.at[own_rows]
        return pltpu.make_async_remote_copy(
            part, part, r_send.at[side], r_recv.at[side],
            device_id=mate_core, device_id_type=MESH)

    def send_sums(r, side, sums):
        r[own_rows, :] = jnp.broadcast_to(sums, (HALF, 128))
        sums_copy(r, side).start()

    def pull(w, side, r, g_ref):
        weights_copy(w, side, 0).wait_recv()
        sums_copy(r, side).wait_recv()
        g_ref[...] = (r[:, 0:1] * s_ref[...].astype(F32)
                      - jnp.dot(w[0], s_ref[...], preferred_element_type=F32))

        def one(k, carry):
            weights_copy(w, side, k + 1).wait_recv()
            g_ref[...] -= jnp.dot(w[k + 1], ms[k], preferred_element_type=F32)
            return carry
        lax.fori_loop(0, ROUNDS, one, 0)

    def mate_s(r, carry):
        wait_bytes(stage_s.at[r], p2_recv.at[S[0], r])
        wait_bytes(stage_r.at[r], p2_recv.at[R[0], r])
        tile_s(r + 1, ms[r])
        return carry

    def mate_u(r, carry):
        wait_bytes(mu.at[r], p2_recv.at[U[0], r])
        tile_u(r + 1, mu[r])
        return carry

    def mate_t(r, carry):
        wait_bytes(stage_a.at[r], p2_recv.at[A[0], r])
        wait_bytes(stage_b.at[r], p2_recv.at[B[0], r])
        tile_t(r + 1, mt[r])
        return carry

    def inverse(k, acc):
        v = 1.0 / ds[k]
        xs[k] = v
        wb[k, own_rows] = v.astype(BF16)
        weights_copy(wb, 1, k).start()
        return acc + jnp.sum(v, axis=1, keepdims=True)

    def deliver_u(*turns):
        @pl.when(holder)
        def _():
            for r in turns:
                deliver(gu, stage_u, mu, U, r, me % 8)

    def deliver_s(r):
        deliver(gs, stage_s, ms, S, r, me)

    def deliver_r(r):
        deliver(gr, stage_r, ms, R, r, me)

    def deliver_a(r):
        deliver(ga, stage_a, mt, A, r, me)

    def deliver_b(r):
        deliver(gb, stage_b, mt, B, r, me)

    scatter(s_ref, gs, S)
    scatter(s_ref, gr, R)
    pl.semaphore_wait(plane_in, 2)
    spread(s_ref, gs, S)
    spread(s_ref, gr, R)
    scatter_u()
    scatter(t_ref, ga, A)
    scatter(t_ref, gb, B)
    tile_s(0, s_ref[...])
    tile_u(0, t_ref[:, SQ:SQ + UQ])
    tile_t(0, t_ref[:, 0:SQ])
    ring(gs, S, 1)
    ring(gr, R, 1)
    ring(gs, S, 2)
    ring(gr, R, 2)
    ring(gs, S, 3)
    ring_u(0)
    ring(gs, S, 4)
    scattered(gs, S)
    deliver_s(0)
    deliver_s(1)
    ring(gr, R, 3)
    deliver_s(2)
    ring_u(1)
    deliver_s(3)
    scattered(ga, A)
    ring(ga, A, 0)
    ring(gr, R, 4)
    scattered(gr, R)
    deliver_r(0)
    deliver_r(1)
    ring_u(2)
    deliver_r(2)
    deliver_r(3)
    ring(ga, A, 1)
    ring_u(3)
    ring(ga, A, 2)
    scattered(gb, B)
    ring(gb, B, 0)
    ring_u(4)
    deliver_u(0)
    deliver_u(1)
    ring(ga, A, 3)
    deliver_u(2)
    ring(gb, B, 1)
    deliver_u(3)
    lax.fori_loop(0, ROUNDS, mate_s, 0)
    ring(ga, A, 4)
    deliver_a(0)
    deliver_a(1)
    ring(gb, B, 2)
    deliver_a(2)
    sum_s = finish(ds, xs, ys, 0)
    wait_bytes(xs, x_send.at[0])
    send_sums(rb, 1, lax.fori_loop(0, TILES, inverse, jnp.zeros((HALF, 1), F32)))
    ring(gb, B, 3)
    deliver_a(3)
    ring(gb, B, 4)
    for r in range(ROUNDS):
        deliver_b(r)
    lax.fori_loop(0, ROUNDS, mate_u, 0)
    pull(wb, 1, rb, gb_ref)
    store_b = pltpu.make_async_copy(gb_ref, gb_hbm, in_sem.at[1])
    store_b.start()
    lax.fori_loop(0, ROUNDS, mate_t, 0)
    sum_t = finish(dt, xt, yt, 1)

    sum_first(0, sum_s, sum_t)
    sum_second(0)
    total_s, total_t = sum_result(0)
    mean_s = total_s / pairs
    inv_s = 1.0 / mean_s
    inv_t = pairs / total_t

    def second(k, carry):
        h, g, acc = carry
        d = ds[k]
        err = d * inv_s - dt[k] * inv_t
        size = jnp.abs(err)
        slope = jnp.clip(err, -1.0, 1.0)
        hub = jnp.where(size < 1.0, 0.5 * err * err, size - 0.5)
        w = slope * xs[k]
        wa[k, own_rows] = w.astype(BF16)
        weights_copy(wa, 0, k).start()
        return (h + jnp.sum(hub, axis=0, keepdims=True),
                g + jnp.sum(slope * d, axis=0, keepdims=True),
                acc + jnp.sum(w, axis=1, keepdims=True))
    zero = jnp.zeros((1, ROWS), F32)
    acc_h, acc_g, sums = lax.fori_loop(0, TILES, second, (zero, zero, jnp.zeros((HALF, 1), F32)))
    sum_first(1, jnp.sum(acc_h, axis=1, keepdims=True), jnp.sum(acc_g, axis=1, keepdims=True))
    send_sums(ra, 0, sums)
    sum_second(1)
    pull(wa, 0, ra, ga_ref)
    store_a = pltpu.make_async_copy(ga_ref, ga_hbm, in_sem.at[0])
    store_a.start()
    total_h, total_g = sum_result(1)
    first = lax.broadcasted_iota(jnp.int32, (8, 128), 0) == 0
    scal_ref[...] = jnp.where(first, total_g / (mean_s * pairs), total_h / pairs)

    store_a.wait()
    store_b.wait()
    for g, piece, stage in ((gs, S, stage_s), (gr, R, stage_r), (ga, A, stage_a),
                            (gb, B, stage_b)):
        wait_bytes(g.at[0, pl.ds(0, NP - 1)], p1_send.at[piece[0]])
        ring_flush(g, piece)
        wait_bytes(stage.at[:, pl.ds(0, NP - 1)], p2_send.at[piece[0]])

    @pl.when(holder)
    def _():
        wait_bytes(gu.at[0, pl.ds(0, 7)], p1_send.at[U[0]])
        ring_flush(gu, U)
        wait_bytes(stage_u.at[:, pl.ds(0, NP - 1)], p2_send.at[U[0]])

    @pl.when(jnp.logical_not(holder))
    def _():
        wait_bytes(gu.at[0, pl.ds(0, 8)], p1_send.at[U[0]])
    wait_bytes(xt, x_send.at[1])
    wait_bytes(wa.at[:, own_rows], w_send.at[0])
    wait_bytes(wb.at[:, own_rows], w_send.at[1])
    sums_copy(ra, 0).wait_send()
    sums_copy(rb, 1).wait_send()
    for n in range(2):
        for half in range(2):
            wait_bytes(pa.at[n, pl.ds(0, NP - 1)], ps_send.at[n, half])


def combine(scal_ref, ga_ref, gb_ref, grad_ref, loss_ref):
    grad_ref[...] = 2.0 * (ga_ref[...] - scal_ref[0, 0] * gb_ref[...])
    loss_ref[0, 0] = scal_ref[1, 0]


def body(student, teacher, rounds):
    pairs = float(NZ * NP * TILES * ROWS * ROWS)
    vmem = pl.BlockSpec(memory_space=pltpu.VMEM)
    smem = pl.BlockSpec(memory_space=pltpu.SMEM)
    hbm = pl.BlockSpec(memory_space=pl.ANY)
    dma = pltpu.SemaphoreType.DMA
    part = jax.ShapeDtypeStruct((ROWS, SQ), F32)
    ga, gb, scal = pl.pallas_call(
        functools.partial(kernel, pairs),
        out_shape=(part, part, jax.ShapeDtypeStruct((8, 128), F32)),
        in_specs=[smem, hbm, hbm],
        out_specs=(hbm, hbm, vmem),
        scratch_shapes=[
            pltpu.VMEM((ROWS, SQ), F32),
            pltpu.VMEM((ROWS, SQ), F32),
            pltpu.VMEM((ROWS, SQ), BF16),
            pltpu.VMEM((ROWS, SQ + UQ), BF16),
            pltpu.VMEM((NZ, NP, VA, CC), BF16),
            pltpu.VMEM((NZ, NP, VB, CC), BF16),
            pltpu.VMEM((NZ, NP, CR, CC), BF16),
            pltpu.VMEM((NZ, NP, VA, CC), BF16),
            pltpu.VMEM((NZ, NP, VB, CC), BF16),
            pltpu.VMEM((ROUNDS, NP, VA, CC), BF16),
            pltpu.VMEM((ROUNDS, NP, VB, CC), BF16),
            pltpu.VMEM((ROUNDS, NP, CR, CC), BF16),
            pltpu.VMEM((ROUNDS, NP, VA, CC), BF16),
            pltpu.VMEM((ROUNDS, NP, VB, CC), BF16),
            pltpu.VMEM((ROUNDS, ROWS, SQ), BF16),
            pltpu.VMEM((ROUNDS, ROWS, SQ), BF16),
            pltpu.VMEM((ROUNDS, ROWS, UQ), BF16),
            pltpu.VMEM((ROWS, 128), F32),
            pltpu.VMEM((ROWS, 128), F32),
            pltpu.VMEM((TILES, HALF, ROWS), F32),
            pltpu.VMEM((TILES, HALF, ROWS), F32),
            pltpu.VMEM((TILES, HALF, ROWS), F32),
            pltpu.VMEM((TILES, HALF, ROWS), F32),
            pltpu.VMEM((TILES, HALF, ROWS), F32),
            pltpu.VMEM((TILES, HALF, ROWS), F32),
            pltpu.VMEM((TILES, ROWS, ROWS), BF16),
            pltpu.VMEM((TILES, ROWS, ROWS), BF16),
            pltpu.VMEM((ROWS, 128), F32),
            pltpu.VMEM((ROWS, 128), F32),
            pltpu.VMEM((2, 2, 1, 128), F32),
            pltpu.VMEM((2, NP, 1, 128), F32),
            pltpu.VMEM((2, NP, 1, 128), F32),
            dma((2,)), pltpu.SemaphoreType.REGULAR,
            dma((5,)), dma((5,)),
            dma((5,)), dma((5, 2, PARTS, NZ // 2)),
            dma((5,)), dma((5, ROUNDS)),
            dma((2,)), dma((2, TILES)),
            dma((2,)), dma((2, TILES)),
            dma((2,)), dma((2,)),
            dma((2, 2)), dma((2, 2)),
        ],
        compiler_params=pltpu.CompilerParams(
            collective_id=0, has_side_effects=True, vmem_limit_bytes=60 * 1024 * 1024),
        name="relation",
    )(rounds, student, teacher)
    grad, loss = pl.pallas_call(
        combine,
        out_shape=(part, jax.ShapeDtypeStruct((1, 1), F32)),
        in_specs=[smem, vmem, vmem],
        out_specs=(vmem, smem),
        name="combine",
    )(scal, ga, gb)
    return grad, loss[0, 0]


def solution(mesh):
    return jax.shard_map(
        body,
        mesh=mesh,
        in_specs=(P("rows", "feat"), P("rows", "feat"), P()),
        out_specs=(P("rows", "feat"), P()),
        check_vma=False,
    )
```

```python
import functools
import jax
import jax.numpy as jnp
from jax import lax
from jax.experimental import pallas as pl
from jax.experimental.pallas import tpu as pltpu
from jax.sharding import PartitionSpec as P

MESH = pl.DeviceIdType.MESH
F32 = jnp.float32
BF16 = jnp.bfloat16
NZ = 8
NP = 16
ROWS = 320
HALF = 160
CR = 80
CC = 128
ROUNDS = 4
TILES = ROUNDS + 1
SQ = 512
UQ = 256
VA = 48
VB = 32
PARTS = 2


def nt_dot(a, b):
    return lax.dot_general(a, b, (((1,), (1,)), ((), ())), preferred_element_type=F32)


def col_norms(m):
    x = m.astype(F32)
    sq = x * x
    hi = sq.astype(BF16)
    lo = (sq - hi.astype(F32)).astype(BF16)
    ones = jnp.ones((8, m.shape[1]), BF16)
    return (nt_dot(ones, hi) + nt_dot(ones, lo))[0:1, :]


def row_norms(m):
    x = m.astype(F32)
    return jnp.sum(x * x, axis=1, keepdims=True)


def wait_bytes(ref, sem):
    pltpu.make_async_copy(ref, ref, sem).wait()


def kernel(pairs, rounds_ref, s_hbm, t_hbm, ga_hbm, gb_hbm, scal_ref, ga_ref, gb_ref,
           s_ref, t_ref, gs, gr, gu, ga, gb, stage_s, stage_r, stage_u, stage_a, stage_b, ms, mt, mu,
           rn_s, rn_t, ds, dt, xs, xt, ys, yt, wa, wb, ra, rb, pv, pa, pb,
           in_sem, plane_in, p1_send, p1_recv, ring_send, ring_recv, p2_send, p2_recv,
           x_send, x_recv, w_send, w_recv, r_send, r_recv, ps_send, ps_recv):
    load_s = pltpu.make_async_copy(s_hbm, s_ref, in_sem.at[0])
    load_t = pltpu.make_async_copy(t_hbm, t_ref, in_sem.at[1])
    load_s.start()
    load_t.start()
    row = lax.axis_index("rows")
    core = lax.axis_index("feat")
    z = row // NP
    me = row % NP
    other = 1 - core
    holder = (me // 8) == core
    base = z * NP

    def plane(d):
        return {"rows": base + d}

    def line(q):
        return {"rows": (q % NZ) * NP + me, "feat": q // NZ}

    q_me = core * NZ + z
    above = ((z + 1) % NZ) * NP
    below = ((z + NZ - 1) % NZ) * NP
    right = {"rows": above + me}
    left = {"rows": below + me}
    mate_core = {"feat": other}

    barrier = pltpu.get_barrier_semaphore()

    def greet(k, carry):
        pl.semaphore_signal(barrier, inc=1, device_id=plane((me + k) % NP), device_id_type=MESH)
        return carry
    lax.fori_loop(1, NP, greet, 0)
    for peer in (right, left, mate_core):
        pl.semaphore_signal(barrier, inc=1, device_id=peer, device_id_type=MESH)
    load_s.wait()
    rn_s[...] = jnp.broadcast_to(row_norms(s_ref[...]), (ROWS, 128))
    load_t.wait()
    rn_t[...] = jnp.broadcast_to(row_norms(t_ref[...]), (ROWS, 128))
    pl.semaphore_wait(barrier, NP + 2)
    for peer in (right, left):
        pl.semaphore_signal(plane_in, inc=1, device_id=peer, device_id_type=MESH)

    S, R, U, A, B = (0, 0, VA), (1, VA, VB), (2, 0, CR), (3, 0, VA), (4, VA, VB)

    def rect(ref, i, piece, first=0):
        r0 = pl.multiple_of((i % 4) * CR + piece[1], 16)
        c0 = pl.multiple_of(first + (i // 4) * CC, CC)
        return ref.at[pl.ds(r0, piece[2]), pl.ds(c0, CC)]

    def scatter(src, g, piece):
        slot = piece[0]

        def one(k, carry):
            d = (me + k) % NP
            pltpu.make_async_remote_copy(
                rect(src, d, piece), g.at[z, me], p1_send.at[slot], p1_recv.at[slot],
                device_id=plane(d), device_id_type=MESH).start()
            return carry
        lax.fori_loop(1, NP, one, 0)
        pltpu.make_async_copy(rect(src, me, piece), g.at[z, me], p1_recv.at[slot]).start()

    def spread(src, g, piece):
        slot = piece[0]

        def one(k, carry):
            d = (me + k) % NP
            for way, first in ((0, above), (1, below)):
                pltpu.make_async_remote_copy(
                    rect(src, d, piece), g.at[z, me],
                    ring_send.at[slot], ring_recv.at[slot, way, me // (NP // PARTS), 0],
                    device_id={"rows": first + d}, device_id_type=MESH).start()
            return carry
        lax.fori_loop(0, NP, one, 0)

    def scatter_u():
        def one(j, carry):
            d = core * 8 + j

            @pl.when(d != me)
            def _():
                pltpu.make_async_remote_copy(
                    rect(t_ref, j, U, SQ), gu.at[z, me], p1_send.at[U[0]], p1_recv.at[U[0]],
                    device_id=plane(d), device_id_type=MESH).start()
            return carry
        lax.fori_loop(0, 8, one, 0)

        @pl.when(holder)
        def _():
            pltpu.make_async_copy(rect(t_ref, me % 8, U, SQ), gu.at[z, me], p1_recv.at[U[0]]).start()

    def scattered(g, piece):
        wait_bytes(g.at[z], p1_recv.at[piece[0]])

    def ring_copy(g, slot, way, part, step):
        block = (z + NZ - step) % NZ if way == 0 else (z + step) % NZ
        ref = g.at[block, pl.ds(part * (NP // PARTS), NP // PARTS)]
        return pltpu.make_async_remote_copy(
            ref, ref, ring_send.at[slot], ring_recv.at[slot, way, part, step],
            device_id=right if way == 0 else left, device_id_type=MESH)

    def ways(part, step):
        return (0, 1) if step < NZ // 2 - 1 else (part // (PARTS // 2),)

    def ring(g, piece, step, parts=range(PARTS)):
        slot = piece[0]
        for part in parts:
            if step > 0:
                for way in ways(part, step - 1):
                    ring_copy(g, slot, way, part, step - 1).wait_recv()
            if step < NZ // 2:
                for way in ways(part, step):
                    ring_copy(g, slot, way, part, step).start()

    def ring_flush(g, piece):
        wait_bytes(g.at[pl.ds(0, NZ - 1)], ring_send.at[piece[0]])

    def ring_u(step):
        @pl.when(holder)
        def _():
            if step == 0:
                scattered(gu, U)
            ring(gu, U, step)

    def deliver(g, stage, mate, piece, r, i):
        slot = piece[0]
        mask = rounds_ref[r]
        zz = z ^ (mask // NP)
        low = mask % NP

        def one(k, carry):
            d = (me + k) % NP
            stage[r, d] = g[zz, d ^ low]

            @pl.when(d != me)
            def _():
                pltpu.make_async_remote_copy(
                    stage.at[r, d], rect(mate.at[r], i, piece), p2_send.at[slot], p2_recv.at[slot, r],
                    device_id=plane(d), device_id_type=MESH).start()

            @pl.when(d == me)
            def _():
                pltpu.make_async_copy(stage.at[r, d], rect(mate.at[r], i, piece), p2_recv.at[slot, r]).start()
            return carry
        lax.fori_loop(1, NP + 1, one, 0)

    own_rows = pl.ds(pl.multiple_of(core * HALF, 16), HALF)
    far_rows = pl.ds(pl.multiple_of(other * HALF, 16), HALF)

    def cross(x, y, side, k):
        return pltpu.make_async_remote_copy(
            x.at[k], y.at[k], x_send.at[side], x_recv.at[side, k],
            device_id=mate_core, device_id_type=MESH)

    def tile_s(k, m):
        cn = col_norms(m)
        xs[k] = rn_s[far_rows, 0:1] + cn - 2.0 * nt_dot(s_ref[far_rows, :], m)
        cross(xs, ys, 0, k).start()
        ds[k] = rn_s[own_rows, 0:1] + cn - 2.0 * nt_dot(s_ref[own_rows, :], m)

    def tile_u(k, m):
        cn = col_norms(m)
        xt[k] = rn_t[far_rows, 0:1] + cn - 2.0 * nt_dot(t_ref[far_rows, SQ:SQ + UQ], m)
        dt[k] = rn_t[own_rows, 0:1] + cn - 2.0 * nt_dot(t_ref[own_rows, SQ:SQ + UQ], m)

    def tile_t(k, m):
        cn = col_norms(m)
        xt[k] += cn - 2.0 * nt_dot(t_ref[far_rows, 0:SQ], m)
        cross(xt, yt, 1, k).start()
        dt[k] += cn - 2.0 * nt_dot(t_ref[own_rows, 0:SQ], m)

    def finish(d, x, y, side):
        def one(k, acc):
            cross(x, y, side, k).wait_recv()
            v = jnp.sqrt(d[k] + y[k] + 1.0)
            d[k] = v
            return acc + jnp.sum(v, axis=0, keepdims=True)
        acc = lax.fori_loop(0, TILES, one, jnp.zeros((1, ROWS), F32))
        return jnp.sum(acc, axis=1, keepdims=True)

    def sum_first(n, a, b):
        first = lax.broadcasted_iota(jnp.int32, (1, 128), 1) == 0
        v = jnp.where(first, a, b)
        pv[n, 0] = v
        pa[n, me] = v

        def send(k, carry):
            pltpu.make_async_remote_copy(
                pv.at[n, 0], pa.at[n, me], ps_send.at[n, 0], ps_recv.at[n, 0],
                device_id=plane((me + k) % NP), device_id_type=MESH).start()
            return carry
        lax.fori_loop(1, NP, send, 0)

    def sum_second(n):
        wait_bytes(pa.at[n, pl.ds(0, NP - 1)], ps_recv.at[n, 0])
        v = jnp.sum(pa[n], axis=0)
        pv[n, 1] = v
        pb[n, q_me] = v

        def send(k, carry):
            pltpu.make_async_remote_copy(
                pv.at[n, 1], pb.at[n, q_me], ps_send.at[n, 1], ps_recv.at[n, 1],
                device_id=line((q_me + k) % NP), device_id_type=MESH).start()
            return carry
        lax.fori_loop(1, NP, send, 0)

    def sum_result(n):
        wait_bytes(pb.at[n, pl.ds(0, NP - 1)], ps_recv.at[n, 1])
        v = jnp.sum(pb[n], axis=0)
        return v[:, 0:1], v[:, 1:2]

    def weights_copy(w, side, k):
        part = w.at[k, own_rows]
        return pltpu.make_async_remote_copy(
            part, part, w_send.at[side], w_recv.at[side, k],
            device_id=mate_core, device_id_type=MESH)

    def sums_copy(r, side):
        part = r.at[own_rows]
        return pltpu.make_async_remote_copy(
            part, part, r_send.at[side], r_recv.at[side],
            device_id=mate_core, device_id_type=MESH)

    def send_sums(r, side, sums):
        r[own_rows, :] = jnp.broadcast_to(sums, (HALF, 128))
        sums_copy(r, side).start()

    def pull(w, side, r, g_ref):
        weights_copy(w, side, 0).wait_recv()
        sums_copy(r, side).wait_recv()
        g_ref[...] = (r[:, 0:1] * s_ref[...].astype(F32)
                      - jnp.dot(w[0], s_ref[...], preferred_element_type=F32))

        def one(k, carry):
            weights_copy(w, side, k + 1).wait_recv()
            g_ref[...] -= jnp.dot(w[k + 1], ms[k], preferred_element_type=F32)
            return carry
        lax.fori_loop(0, ROUNDS, one, 0)

    def mate_s(r, carry):
        wait_bytes(stage_s.at[r], p2_recv.at[S[0], r])
        wait_bytes(stage_r.at[r], p2_recv.at[R[0], r])
        tile_s(r + 1, ms[r])
        return carry

    def mate_u(r, carry):
        wait_bytes(mu.at[r], p2_recv.at[U[0], r])
        tile_u(r + 1, mu[r])
        return carry

    def mate_t(r, carry):
        wait_bytes(stage_a.at[r], p2_recv.at[A[0], r])
        wait_bytes(stage_b.at[r], p2_recv.at[B[0], r])
        tile_t(r + 1, mt[r])
        return carry

    def inverse(k, acc):
        v = 1.0 / ds[k]
        xs[k] = v
        wb[k, own_rows] = v.astype(BF16)
        weights_copy(wb, 1, k).start()
        return acc + jnp.sum(v, axis=1, keepdims=True)

    def deliver_u(*turns):
        @pl.when(holder)
        def _():
            for r in turns:
                deliver(gu, stage_u, mu, U, r, me % 8)

    def deliver_s(r):
        deliver(gs, stage_s, ms, S, r, me)

    def deliver_r(r):
        deliver(gr, stage_r, ms, R, r, me)

    def deliver_a(r):
        deliver(ga, stage_a, mt, A, r, me)

    def deliver_b(r):
        deliver(gb, stage_b, mt, B, r, me)

    scatter(s_ref, gs, S)
    scatter(s_ref, gr, R)
    pl.semaphore_wait(plane_in, 2)
    spread(s_ref, gs, S)
    spread(s_ref, gr, R)
    scatter_u()
    scatter(t_ref, ga, A)
    scatter(t_ref, gb, B)
    tile_s(0, s_ref[...])
    tile_u(0, t_ref[:, SQ:SQ + UQ])
    tile_t(0, t_ref[:, 0:SQ])
    ring(gs, S, 1)
    ring(gr, R, 1)
    ring(gs, S, 2)
    ring(gr, R, 2)
    ring(gs, S, 3)
    ring_u(0)
    ring(gs, S, 4)
    scattered(gs, S)
    deliver_s(0)
    deliver_s(1)
    ring(gr, R, 3)
    deliver_s(2)
    ring_u(1)
    deliver_s(3)
    scattered(ga, A)
    ring(ga, A, 0)
    ring(gr, R, 4)
    scattered(gr, R)
    deliver_r(0)
    deliver_r(1)
    ring_u(2)
    deliver_r(2)
    deliver_r(3)
    ring(ga, A, 1)
    ring_u(3)
    ring(ga, A, 2)
    scattered(gb, B)
    ring(gb, B, 0)
    ring_u(4)
    deliver_u(0)
    deliver_u(1)
    ring(ga, A, 3)
    deliver_u(2)
    ring(gb, B, 1)
    deliver_u(3)
    lax.fori_loop(0, ROUNDS, mate_s, 0)
    ring(ga, A, 4)
    deliver_a(0)
    deliver_a(1)
    ring(gb, B, 2)
    deliver_a(2)
    sum_s = finish(ds, xs, ys, 0)
    wait_bytes(xs, x_send.at[0])
    send_sums(rb, 1, lax.fori_loop(0, TILES, inverse, jnp.zeros((HALF, 1), F32)))
    ring(gb, B, 3)
    deliver_a(3)
    ring(gb, B, 4)
    for r in range(ROUNDS):
        deliver_b(r)
    lax.fori_loop(0, ROUNDS, mate_u, 0)
    pull(wb, 1, rb, gb_ref)
    store_b = pltpu.make_async_copy(gb_ref, gb_hbm, in_sem.at[1])
    store_b.start()
    lax.fori_loop(0, ROUNDS, mate_t, 0)
    sum_t = finish(dt, xt, yt, 1)

    sum_first(0, sum_s, sum_t)
    sum_second(0)
    total_s, total_t = sum_result(0)
    mean_s = total_s / pairs
    inv_s = 1.0 / mean_s
    inv_t = pairs / total_t

    def second(k, carry):
        h, g, acc = carry
        d = ds[k]
        err = d * inv_s - dt[k] * inv_t
        size = jnp.abs(err)
        slope = jnp.clip(err, -1.0, 1.0)
        hub = jnp.where(size < 1.0, 0.5 * err * err, size - 0.5)
        w = slope * xs[k]
        wa[k, own_rows] = w.astype(BF16)
        weights_copy(wa, 0, k).start()
        return (h + jnp.sum(hub, axis=0, keepdims=True),
                g + jnp.sum(slope * d, axis=0, keepdims=True),
                acc + jnp.sum(w, axis=1, keepdims=True))
    zero = jnp.zeros((1, ROWS), F32)
    acc_h, acc_g, sums = lax.fori_loop(0, TILES, second, (zero, zero, jnp.zeros((HALF, 1), F32)))
    sum_first(1, jnp.sum(acc_h, axis=1, keepdims=True), jnp.sum(acc_g, axis=1, keepdims=True))
    send_sums(ra, 0, sums)
    sum_second(1)
    pull(wa, 0, ra, ga_ref)
    store_a = pltpu.make_async_copy(ga_ref, ga_hbm, in_sem.at[0])
    store_a.start()
    total_h, total_g = sum_result(1)
    first = lax.broadcasted_iota(jnp.int32, (8, 128), 0) == 0
    scal_ref[...] = jnp.where(first, total_g / (mean_s * pairs), total_h / pairs)

    store_a.wait()
    store_b.wait()
    for g, piece, stage in ((gs, S, stage_s), (gr, R, stage_r), (ga, A, stage_a),
                            (gb, B, stage_b)):
        wait_bytes(g.at[0, pl.ds(0, NP - 1)], p1_send.at[piece[0]])
        ring_flush(g, piece)
        wait_bytes(stage.at[:, pl.ds(0, NP - 1)], p2_send.at[piece[0]])

    @pl.when(holder)
    def _():
        wait_bytes(gu.at[0, pl.ds(0, 7)], p1_send.at[U[0]])
        ring_flush(gu, U)
        wait_bytes(stage_u.at[:, pl.ds(0, NP - 1)], p2_send.at[U[0]])

    @pl.when(jnp.logical_not(holder))
    def _():
        wait_bytes(gu.at[0, pl.ds(0, 8)], p1_send.at[U[0]])
    wait_bytes(xt, x_send.at[1])
    wait_bytes(wa.at[:, own_rows], w_send.at[0])
    wait_bytes(wb.at[:, own_rows], w_send.at[1])
    sums_copy(ra, 0).wait_send()
    sums_copy(rb, 1).wait_send()
    for n in range(2):
        for half in range(2):
            wait_bytes(pa.at[n, pl.ds(0, NP - 1)], ps_send.at[n, half])


def combine(scal_ref, ga_ref, gb_ref, grad_ref, loss_ref):
    grad_ref[...] = 2.0 * (ga_ref[...] - scal_ref[0, 0] * gb_ref[...])
    loss_ref[0, 0] = scal_ref[1, 0]


def body(student, teacher, rounds):
    pairs = float(NZ * NP * TILES * ROWS * ROWS)
    vmem = pl.BlockSpec(memory_space=pltpu.VMEM)
    smem = pl.BlockSpec(memory_space=pltpu.SMEM)
    hbm = pl.BlockSpec(memory_space=pl.ANY)
    dma = pltpu.SemaphoreType.DMA
    part = jax.ShapeDtypeStruct((ROWS, SQ), F32)
    ga, gb, scal = pl.pallas_call(
        functools.partial(kernel, pairs),
        out_shape=(part, part, jax.ShapeDtypeStruct((8, 128), F32)),
        in_specs=[smem, hbm, hbm],
        out_specs=(hbm, hbm, vmem),
        scratch_shapes=[
            pltpu.VMEM((ROWS, SQ), F32),
            pltpu.VMEM((ROWS, SQ), F32),
            pltpu.VMEM((ROWS, SQ), BF16),
            pltpu.VMEM((ROWS, SQ + UQ), BF16),
            pltpu.VMEM((NZ, NP, VA, CC), BF16),
            pltpu.VMEM((NZ, NP, VB, CC), BF16),
            pltpu.VMEM((NZ, NP, CR, CC), BF16),
            pltpu.VMEM((NZ, NP, VA, CC), BF16),
            pltpu.VMEM((NZ, NP, VB, CC), BF16),
            pltpu.VMEM((ROUNDS, NP, VA, CC), BF16),
            pltpu.VMEM((ROUNDS, NP, VB, CC), BF16),
            pltpu.VMEM((ROUNDS, NP, CR, CC), BF16),
            pltpu.VMEM((ROUNDS, NP, VA, CC), BF16),
            pltpu.VMEM((ROUNDS, NP, VB, CC), BF16),
            pltpu.VMEM((ROUNDS, ROWS, SQ), BF16),
            pltpu.VMEM((ROUNDS, ROWS, SQ), BF16),
            pltpu.VMEM((ROUNDS, ROWS, UQ), BF16),
            pltpu.VMEM((ROWS, 128), F32),
            pltpu.VMEM((ROWS, 128), F32),
            pltpu.VMEM((TILES, HALF, ROWS), F32),
            pltpu.VMEM((TILES, HALF, ROWS), F32),
            pltpu.VMEM((TILES, HALF, ROWS), F32),
            pltpu.VMEM((TILES, HALF, ROWS), F32),
            pltpu.VMEM((TILES, HALF, ROWS), F32),
            pltpu.VMEM((TILES, HALF, ROWS), F32),
            pltpu.VMEM((TILES, ROWS, ROWS), BF16),
            pltpu.VMEM((TILES, ROWS, ROWS), BF16),
            pltpu.VMEM((ROWS, 128), F32),
            pltpu.VMEM((ROWS, 128), F32),
            pltpu.VMEM((2, 2, 1, 128), F32),
            pltpu.VMEM((2, NP, 1, 128), F32),
            pltpu.VMEM((2, NP, 1, 128), F32),
            dma((2,)), pltpu.SemaphoreType.REGULAR,
            dma((5,)), dma((5,)),
            dma((5,)), dma((5, 2, PARTS, NZ // 2)),
            dma((5,)), dma((5, ROUNDS)),
            dma((2,)), dma((2, TILES)),
            dma((2,)), dma((2, TILES)),
            dma((2,)), dma((2,)),
            dma((2, 2)), dma((2, 2)),
        ],
        compiler_params=pltpu.CompilerParams(
            collective_id=0, has_side_effects=True, vmem_limit_bytes=60 * 1024 * 1024),
        name="relation",
    )(rounds, student, teacher)
    grad, loss = pl.pallas_call(
        combine,
        out_shape=(part, jax.ShapeDtypeStruct((1, 1), F32)),
        in_specs=[smem, vmem, vmem],
        out_specs=(vmem, smem),
        name="combine",
    )(scal, ga, gb)
    return grad, loss[0, 0]


def solution(mesh):
    return jax.shard_map(
        body,
        mesh=mesh,
        in_specs=(P("rows", "feat"), P("rows", "feat"), P()),
        out_specs=(P("rows", "feat"), P()),
        check_vma=False,
    )
```
